32 devices in a mesh: groups: 2 (over y), expert: 4 (over z), node: 2 (over x), inner: 2 (over core).
Axes of the slice: x: 2, y: 2, z: 4, core: 2. Of those that a mesh axis runs over, the one named last changes fastest.
Arguments:
- tokens: bfloat16 [2048, 2048], P(('groups', 'expert', 'node', 'inner')), parts along dimension 0, may hold values from -6 to 6
- slot_choice: int32 [2048, 8], P(('groups', 'expert', 'node', 'inner')), parts along dimension 0, may hold values from 0 to 15, all different within a row; in each aligned block of 64 rows (0 to 63, 64 to 127, ...) at most 64 rows name the same one
- gate_fixed: int32 [2048, 8], P(('groups', 'expert', 'node', 'inner')), parts along dimension 0, may hold values from 1 to 65536
- expert_gate: bfloat16 [8, 2048, 384], P(('expert', 'node')), may hold values from -0.125 to 0.125
- expert_up: bfloat16 [8, 2048, 384], P(('expert', 'node')), may hold values from -0.125 to 0.125
- expert_down: bfloat16 [8, 384, 2048], P(('expert', 'node')), may hold values from -0.3125 to 0.3125
- next_weights: bfloat16 [8, 3, 2048, 384], P(('expert', 'node'), None, 'inner'), may hold values from -6 to 6
- hot_expert: int32 [4], P('groups'), parts along dimension 0, may hold values from 0 to 7, as said below
- slot_take: int32 [32], P(('groups', 'expert', 'node', 'inner')), parts along dimension 0, may hold values from 0 to 2
Outputs:
- moe_out: bfloat16 [2048, 2048], P(('groups', 'expert', 'node', 'inner')), parts along dimension 0
- new_weights: bfloat16 [32, 3, 2048, 384], P(('groups', 'expert', 'node', 'inner')), parts along dimension 0
The draws below stay inside these ranges and needn't reach their ends.
There are 2 independent parts, one for each index of `groups`. The reference program is written for one: setup_inputs(seed, part) draws one part's arguments, and reference() takes and returns one part's arrays. A program takes and returns all parts, laid end to end along the dimension named above; an argument that names none is the same for every part. Nothing has to cross between parts.
Inputs may be any that keep to these rules, and one draw needn't show every extreme that they name: `slot_choice`: a token's 8 slots differ; at most 64 of the pairs of one device's tokens name one slot, and in every draw some device names some slot exactly 64 times. `hot_expert`: the 2 entries are different experts; expert 8 - 1 is always one of them.
All inputs are finite; a program needn't handle non-finite values.
Results may differ from the reference program's by a relative error of at most 0.0058.
Values may be sent and summed in bfloat16 or wider, within the bound.
A program may use at most 128 MiB of HBM per device.

```python
import math
import jax
import jax.numpy as jnp
import numpy as np
from jax import lax

D = 2048
FF = 384
TOP = 8
HOT = 2
TOK_DEV = 64
EXPERTS = 8
SLOTS = 16
CAP = 64
TOKENS = 1024
N_EXPERT = 4
N_NODE = 2
N_INNER = 2


def draw_hot_expert(key, part):
    others = jax.random.permutation(jax.random.fold_in(key, 7), EXPERTS - 1)[:HOT - 1].astype(jnp.int32)
    offset = jax.random.randint(jax.random.fold_in(key, 11), (), 0, HOT).astype(jnp.int32)
    place = ((offset * 0 + jnp.asarray(part).astype(jnp.int32)) % HOT).astype(jnp.int32)
    position = jnp.arange(HOT, dtype=jnp.int32)
    other_index = jnp.clip(position - (position > place).astype(jnp.int32), 0, HOT - 2)
    chosen = jnp.where(position == place, jnp.int32(EXPERTS - 1), others[other_index])
    return chosen.astype(jnp.int32)


def set_ends(array, rng, low, top_value):
    longest = array.shape.index(max(array.shape))
    spots = []
    for shift in (0, 1):
        where = [jax.random.randint(jax.random.fold_in(rng, axis), (), 0, length) for axis, length in enumerate(array.shape)]
        where[longest] = (where[longest] + shift) % array.shape[longest]
        spots.append(tuple(where))
    return array.at[spots[0]].set(low).at[spots[1]].set(top_value)


def shard_levels(key, extent, shards, least, high):
    loudness, own = 1.0, jax.random.fold_in(key, 6)
    for dim, parts in shards:
        draws = jnp.exp(jax.random.uniform(jax.random.fold_in(own, dim), (parts,), jnp.float32, least / len(shards), high / len(shards)))
        loudness = loudness * jnp.repeat(draws, extent[dim] // parts).reshape([-1 if axis == dim else 1 for axis in range(len(extent))])
    return loudness


def assign_block(own_key, own, number, rows, count, top, bound, skew):
    ranking = jax.random.permutation(own_key, count)
    crowded, usual = portions_of(count, rows * top, bound, skew, True), portions_of(count, rows * top, bound, skew, False)
    places = jnp.arange(count)

    def named(sizes, turn):
        used = int((sizes > 0).sum())
        fixed = max(1, used // 4)
        moved = fixed + (places - fixed + turn * (used - fixed)) % max(1, count - fixed)
        return jnp.zeros((count,), jnp.int32).at[ranking[jnp.where(places < fixed, places, moved)]].set(jnp.asarray(sizes, jnp.int32))

    sizes = jnp.where(number % 4 == 0, named(crowded, number // 4), named(usual, number - number // 4 - 1))
    mixed = jax.random.permutation(jax.random.fold_in(own, 3), count)
    source_of, sink = mixed[0:count // 2 * 2:2], mixed[1:count // 2 * 2:2]
    margin = jnp.minimum(sizes[source_of] - 1, bound - sizes[sink]) // 2
    margin = jnp.where((source_of == ranking[0]) | (sink == ranking[0]) | (sizes[sink] == 0), 0, jnp.maximum(margin, 0))
    moved = jax.random.randint(jax.random.fold_in(own, 4), (count // 2,), 0, 1 << 20) % (margin + 1)
    sizes = sizes.at[source_of].add(-moved).at[sink].add(moved)
    labels = jnp.searchsorted(jnp.cumsum(sizes), jnp.arange(rows * top), side="right").astype(jnp.int32)
    listing = labels.reshape(top, rows).T
    listing = listing[jax.random.permutation(jax.random.fold_in(own, 1), rows)]
    turn = jax.random.randint(jax.random.fold_in(own, 2), (rows, 1), 0, top)
    return jnp.take_along_axis(listing, (jnp.arange(top)[None, :] + turn) % top, axis=1)


def portions_of(number_of, total, reach, slope, full):
    portions = [(1 << 20) // math.isqrt(grade ** slope) + 1 for grade in range(1, number_of + 1)]
    largest = reach if full else min(reach, max(-(-total // number_of), total * portions[0] // sum(portions)))
    least = 1 if total - largest >= number_of - 1 else 0
    given, spare = [largest] + [least] * (number_of - 1), total - largest - least * (number_of - 1)
    while spare > 0:
        candidates = [i for i in range(1, number_of) if given[i] < largest] or [i for i in range(1, number_of) if given[i] < reach]
        pool, remaining = sum([portions[i] for i in candidates]), spare
        for i in candidates:
            more = min(reach - given[i], max(1, remaining * portions[i] // pool), spare)
            given[i] = given[i] + more
            spare = spare - more
    return np.array(given)


def noise(stream_key, shape, scale, limit, cuts=(), kind=jnp.bfloat16):
    loudness = shard_levels(stream_key, shape, cuts, -0.22, 0.18) if cuts else 1.0
    drawn = jax.random.normal(stream_key, shape, jnp.float32) * scale * loudness
    return jnp.minimum(jnp.maximum(drawn, -limit), limit).astype(kind)


def setup_inputs(seed: int = 0, part: int = 0) -> dict:
    keys = jax.random.split(jax.random.key(seed), 10)
    part_splits = jax.random.split(jax.random.fold_in(keys[9], part), 10)
    tokens = noise(part_splits[0], (TOKENS, D), 1.0, 6.0, ((0, 16),))
    slot_choice_keys = jax.random.split(jax.random.fold_in(part_splits[1], 1), TOKENS // TOK_DEV)
    slot_choice_turns = jax.random.permutation(jax.random.fold_in(part_splits[1], 3), TOKENS // TOK_DEV)
    slot_choice = jax.vmap(lambda own, number: assign_block(jax.random.fold_in(part_splits[1], 2), own, number, TOK_DEV, SLOTS, TOP, CAP, 1))(slot_choice_keys, slot_choice_turns).reshape((TOKENS, TOP))
    gate_fixed = set_ends(jax.random.randint(part_splits[2], (TOKENS, TOP), 1, 65537), jax.random.fold_in(part_splits[2], 1), 1, 65536).astype(jnp.int32)
    expert_gate = noise(keys[3], (EXPERTS, D, FF), D ** -0.5, 0.125, ((0, 8),))
    expert_up = noise(keys[4], (EXPERTS, D, FF), D ** -0.5, 0.125, ((0, 8),))
    expert_down = noise(keys[5], (EXPERTS, FF, D), FF ** -0.5, 0.3125, ((0, 8),))
    next_weights = noise(keys[6], (EXPERTS, 3, D, FF), 1.0, 6.0, ((0, 8), (2, 2)))
    hot_expert = draw_hot_expert(jax.random.fold_in(jax.random.fold_in(keys[9], part), 71), part)
    slot_take = set_ends(jax.random.randint(part_splits[8], (SLOTS,), 0, HOT + 1), jax.random.fold_in(part_splits[8], 1), 0, HOT).astype(jnp.int32)
    return {"tokens": tokens, "slot_choice": slot_choice, "gate_fixed": gate_fixed, "expert_gate": expert_gate, "expert_up": expert_up, "expert_down": expert_down, "next_weights": next_weights, "hot_expert": hot_expert, "slot_take": slot_take}


def reference(tokens, slot_choice, gate_fixed, expert_gate, expert_up, expert_down, next_weights, hot_expert, slot_take):
    slot_count = N_EXPERT * N_NODE * N_INNER
    pair_slot = slot_choice.reshape(-1).astype(jnp.int32)
    pair_expert = (pair_slot // N_INNER).astype(jnp.int32)
    sorted_pairs = jnp.argsort(pair_expert, stable=True).astype(jnp.int32)
    expert_ids = jnp.arange(EXPERTS, dtype=jnp.int32)
    counts = jnp.sum((pair_expert[:, None] == expert_ids[None, :]).astype(jnp.int32), axis=0).astype(jnp.int32)
    starts = (jnp.cumsum(counts) - counts).astype(jnp.int32)
    rows_most = N_INNER * slot_count * CAP
    padded_pairs = jnp.concatenate([sorted_pairs, jnp.zeros((rows_most,), jnp.int32)])
    factors = gate_fixed.reshape(-1).astype(jnp.float32) / 65536.0

    def expert_step(accumulated, expert):
        picked = lax.dynamic_slice_in_dim(padded_pairs, starts[expert], rows_most)
        live_row = jnp.arange(rows_most, dtype=jnp.int32) < counts[expert]
        token_index = (picked // TOP).astype(jnp.int32)
        block_rows = tokens[token_index]
        gate_value = jnp.dot(block_rows, expert_gate[expert], preferred_element_type=jnp.float32)
        up_value = jnp.dot(block_rows, expert_up[expert], preferred_element_type=jnp.float32)
        hidden = (jax.nn.silu(gate_value) * up_value).astype(jnp.bfloat16)
        result = jnp.dot(hidden, expert_down[expert], preferred_element_type=jnp.float32).astype(jnp.bfloat16)
        result = lax.optimization_barrier(result).astype(jnp.float32)
        factor = jnp.where(live_row, factors[picked], jnp.float32(0.0))
        return accumulated.at[token_index].add(result * factor[:, None]), None

    accumulated, unused = lax.scan(expert_step, jnp.zeros((TOKENS, D), jnp.float32), expert_ids)
    moe_out = accumulated.astype(jnp.bfloat16)
    hot_pick = hot_expert[jnp.minimum(slot_take, HOT - 1)]
    copied = next_weights[hot_pick]
    new_weights = jnp.where((slot_take < HOT)[:, None, None, None], copied, jnp.zeros_like(copied))
    return moe_out, new_weights
```

```python
import functools

import jax
import jax.numpy as jnp
from jax import lax
from jax.experimental import pallas as pl
from jax.experimental.pallas import tpu as pltpu
from jax.sharding import PartitionSpec as P

MESH = pl.DeviceIdType.MESH
BF16 = jnp.bfloat16
F32 = jnp.float32
KINDS = 3


def routed(tokens, slot_choice, gate_fixed, expert_gate, expert_up, expert_down):
    slot_count = lax.axis_size(("expert", "node", "inner"))
    tok_rows, model_width = tokens.shape
    pick_count = slot_choice.shape[1]
    capacity = max(2, 2 * tok_rows * pick_count // slot_count)
    flat_slot = slot_choice.reshape(-1)
    columns = jnp.arange(slot_count, dtype=jnp.int32)
    onehot = (flat_slot[:, None] == columns[None, :]).astype(jnp.int32)
    before = jnp.cumsum(onehot, axis=0) - onehot
    position = jnp.sum(before * onehot, axis=1)
    target = flat_slot * capacity + position
    source_rows = jnp.repeat(tokens, pick_count, axis=0)
    outgoing = jnp.zeros((slot_count * capacity, model_width), BF16).at[target].set(source_rows)
    outgoing = outgoing.reshape(slot_count, capacity, model_width)
    axes = ("expert", "node", "inner")
    block_rows = lax.all_to_all(outgoing, axes, split_axis=0, concat_axis=0, tiled=True)
    flat_rows = block_rows.reshape(-1, model_width)
    gate_value = jnp.dot(flat_rows, expert_gate[0], preferred_element_type=F32)
    up_value = jnp.dot(flat_rows, expert_up[0], preferred_element_type=F32)
    hidden = (jax.nn.silu(gate_value) * up_value).astype(BF16)
    result = jnp.dot(hidden, expert_down[0], preferred_element_type=F32).astype(BF16)
    returned = lax.all_to_all(
        result.reshape(block_rows.shape), axes, split_axis=0, concat_axis=0, tiled=True
    )
    back_rows = returned.reshape(slot_count * capacity, model_width)[target]
    factors = gate_fixed.reshape(-1).astype(F32) * (1.0 / 65536.0)
    weighted = back_rows.astype(F32) * factors[:, None]
    return jnp.sum(weighted.reshape(tok_rows, pick_count, model_width), axis=1).astype(BF16)


def pick(condition, yes, no):
    return lax.select_n(condition, no, yes)


def kernel(sizes, dense, *refs):
    ng, nz, nx, ni = sizes
    refs = list(refs)
    nw, hot, take = refs[:3]
    del refs[:3]
    if dense:
        tokens, factors, w_gate, w_up, w_down = refs[:5]
        del refs[:5]
        moe_out = refs.pop(0)
    out = refs.pop(0)
    (meta, meta_y, meta_i, xin, up, dn, full, own_out, peer_out) = refs[:9]
    del refs[:9]
    (m_send, m_recv, s1s, s1r, ups, upr, dns, dnr, xs, xr, ys, yr, os, ps, pr) = refs[:15]
    del refs[:15]

    g, z, x, i = (lax.axis_index(a) for a in ("groups", "expert", "node", "inner"))
    half = nw.shape[2]
    part = half // (nx * ng)
    experts = nz * nx
    unions = 1 + ng
    items = KINDS * unions
    above, below = lax.rem(z + 1, nz), lax.rem(z + nz - 1, nz)

    def rows(p, q):
        return pl.ds(pl.multiple_of((p * ng + q) * part, part), part)

    def remote(src, dst, send, recv, **where):
        return pltpu.make_async_remote_copy(
            src_ref=src, dst_ref=dst, send_sem=send, recv_sem=recv, device_id=where, device_id_type=MESH
        )

    barrier = pltpu.get_barrier_semaphore()

    def greet(**where):
        pl.semaphore_signal(barrier, inc=1, device_id=where, device_id_type=MESH)

    for d in range(1, nx):
        greet(node=lax.rem(x + d, nx))
    for d in range(1, ng):
        greet(groups=lax.rem(g + d, ng))
    for d in range(1, ni):
        greet(inner=lax.rem(i + d, ni))

    @pl.when(z > 0)
    def _():
        greet(expert=below)

    @pl.when(z < nz - 1)
    def _():
        greet(expert=above)

    ends = (z > 0).astype(jnp.int32) + (z < nz - 1).astype(jnp.int32)
    pl.semaphore_wait(barrier, nx - 1 + ng - 1 + ni - 1 + ends)

    last = experts - 1
    other = hot[0] + hot[1] - last
    last_place = pick(hot[0] == last, jnp.int32(0), jnp.int32(1))
    code = pick(take[0] == 2, jnp.int32(2), pick(take[0] == last_place, jnp.int32(0), jnp.int32(1)))
    line = lax.broadcasted_iota(jnp.int32, meta.shape, 0)
    meta[...] = jnp.where(line == 0, other, code)
    meta_copies = []
    for d in range(1, ng):
        n = len(meta_copies)
        meta_copies.append(
            remote(meta, meta_y.at[d - 1], m_send.at[n], m_recv.at[n], groups=lax.rem(g + d, ng))
        )
    for d in range(1, ni):
        n = len(meta_copies)
        meta_copies.append(
            remote(meta, meta_i.at[d - 1], m_send.at[n], m_recv.at[n], inner=lax.rem(i + d, ni))
        )
    for copy in meta_copies:
        copy.start()

    if dense:
        (tok, fac, acc, res, xres, rup, rdn) = refs[:7]
        (tus, tur, tds, tdr, txs, txr, fus, fur, fds, fdr, fxs, fxr, rxs, rxr, rus, rur, rds, rdr) = refs[7:]
        tok_rows = tokens.shape[0]

        def tok_up(b):
            return [
                remote(tok.at[x, b], tok.at[x, b], tus.at[b], tur.at[b], expert=above),
                remote(fac.at[x, b], fac.at[x, b], fus.at[b], fur.at[b], expert=above),
            ]

        def tok_dn(b):
            return [
                remote(tok.at[x, b], tok.at[x, b], tds.at[b], tdr.at[b], expert=below),
                remote(fac.at[x, b], fac.at[x, b], fds.at[b], fdr.at[b], expert=below),
            ]

        def tok_x(d, b, col):
            to = lax.rem(x + d, nx)
            return [
                remote(tok.at[col, b], tok.at[col, b], txs.at[d - 1, b], txr.at[d - 1, b], node=to),
                remote(fac.at[col, b], fac.at[col, b], fxs.at[d - 1, b], fxr.at[d - 1, b], node=to),
            ]

        tok[x, z] = tokens[...]
        fac[x, z] = factors[...]

        def tok_step(s, carry):
            bu, bd = z - s, z + s

            @pl.when(bu >= 0)
            def _():
                @pl.when(s > 0)
                def _():
                    for c in tok_up(bu):
                        c.wait_recv()

                @pl.when(z < nz - 1)
                def _():
                    for c in tok_up(bu):
                        c.start()

                for d in range(1, nx):
                    for c in tok_x(d, bu, x):
                        c.start()

            @pl.when(bd < nz)
            def _():
                @pl.when(s > 0)
                def _():
                    for c in tok_dn(bd):
                        c.wait_recv()

                @pl.when(z > 0)
                def _():
                    for c in tok_dn(bd):
                        c.start()

                @pl.when(s > 0)
                def _():
                    for d in range(1, nx):
                        for c in tok_x(d, bd, x):
                            c.start()

            return carry

    def first(d, k):
        to = lax.rem(x + d, nx)
        return remote(nw.at[0, k, rows(to, g)], xin.at[d - 1, k], s1s.at[d - 1, k], s1r.at[d - 1, k], node=to)

    def start_first():
        for k in range(KINDS):
            for d in range(1, nx):
                first(d, k).start()

    def up_copy(j):
        return remote(up.at[j], up.at[j], ups.at[j], upr.at[j], expert=above)

    def dn_copy(j):
        return remote(dn.at[j], dn.at[j], dns.at[j], dnr.at[j], expert=below)

    def x_copy(d, j, p):
        k, u = j // unions, j % unions
        spot = full.at[u, k, p, g]
        return remote(spot, spot, xs.at[d - 1, j], xr.at[d - 1, j], node=lax.rem(x + d, nx))

    def y_copy(d, j, p, q):
        k, u = j // unions, j % unions
        spot = full.at[u, k, p, q]
        return remote(spot, spot, ys.at[d - 1, j, p], yr.at[d - 1, j, p], groups=lax.rem(g + d, ng))

    def y_wanted(d, j):
        u = j % unions
        return (u == 0) | (u == 1 + lax.rem(g + d, ng))

    def y_start(j, p):
        for d in range(1, ng):
            @pl.when(y_wanted(d, j))
            def _():
                y_copy(d, j, p, g).start()

    def hot_loop():
        others = [other] + [jnp.max(meta_y[d - 1, 0:1, :]) for d in range(1, ng)]

        def owner(u):
            expert = jnp.int32(last)
            for d in range(ng):
                expert = pick(u == 1 + lax.rem(g + ng - d, ng), others[d], expert)
            return expert // nx, expert % nx

        def here(j):
            k, u = j // unions, j % unions
            oz, ox = owner(u)
            value = nw[0, k, rows(x, g), :]
            for d in range(1, nx):
                value = pick(ox == lax.rem(x + nx - d, nx), xin[d - 1, k], value)
            return oz, value

        def line_step(j, buffer, copy, first_one, last_one):
            @pl.when((j >= 0) & (j < items))
            def _():
                oz, value = here(j)

                @pl.when(first_one)
                def _():
                    buffer[j] = value

                @pl.when(jnp.logical_not(first_one))
                def _():
                    copy(j).wait_recv()
                    buffer[j] = pick(oz == z, value, buffer[j])

                @pl.when(jnp.logical_not(last_one))
                def _():
                    copy(j).start()

        lag = 2
        far = jnp.maximum(z, nz - 1 - z)

        def step(s, carry):
            line_step(s - z, up, up_copy, z == 0, z == nz - 1)
            line_step(s - (nz - 1 - z), dn, dn_copy, z == nz - 1, z == 0)
            j = s - far

            @pl.when((j >= 0) & (j < items))
            def _():
                k, u = j // unions, j % unions
                oz, _ = owner(u)
                full[u, k, x, g] = pick(oz <= z, up[j], dn[j])
                for d in range(1, nx):
                    x_copy(d, j, x).start()
                y_start(j, x)

            j2 = j - lag

            @pl.when((j2 >= 0) & (j2 < items))
            def _():
                for d in range(1, nx):
                    p = lax.rem(x + nx - d, nx)
                    x_copy(d, j2, p).wait_recv()
                    y_start(j2, p)

            return carry

        lax.fori_loop(0, items + nz - 1 + lag, step, 0)

    def out_rows():
        return pl.ds(pl.multiple_of(i * half, half), half)

    def own_copy(k):
        return pltpu.make_async_copy(own_out.at[k], out.at[0, k, out_rows()], os.at[k])

    def peer_copy(d, k):
        to = lax.rem(i + d, ni)
        return remote(peer_out.at[d - 1, k], out.at[0, k, out_rows()], ps.at[d - 1, k], pr.at[d - 1, k], inner=to)

    def finish_hot():
        codes = [jnp.max(meta_i[d - 1, 1:2, :]) for d in range(1, ni)]
        for k in range(KINDS):
            for d in range(1, ng):
                q = lax.rem(g + ng - d, ng)
                for p in range(nx):
                    y_copy(d, k * unions, p, q).wait_recv()
                    y_copy(d, k * unions + 1 + g, p, q).wait_recv()
            known = full[0, k].reshape(half, full.shape[-1])
            second = full[1 + g, k].reshape(half, full.shape[-1])

            def chosen(c):
                return pick(c == 2, jnp.zeros_like(known), pick(c == 0, known, second))

            for d in range(1, ni):
                peer_out[d - 1, k] = chosen(codes[ni - d - 1])
                peer_copy(d, k).start()
            own_out[k] = chosen(code)
            own_copy(k).start()

    def drain():
        for copy in meta_copies:
            copy.wait_send()
        for k in range(KINDS):
            for d in range(1, nx):
                first(d, k).wait_send()

        def sends(j, carry):
            @pl.when(z < nz - 1)
            def _():
                up_copy(j).wait_send()

            @pl.when(z > 0)
            def _():
                dn_copy(j).wait_send()

            for d in range(1, nx):
                x_copy(d, j, x).wait_send()
            for d in range(1, ng):
                @pl.when(y_wanted(d, j))
                def _():
                    for p in range(nx):
                        y_copy(d, j, p, g).wait_send()
            return carry

        lax.fori_loop(0, items, sends, 0)
        for k in range(KINDS):
            own_copy(k).wait()
            for d in range(1, ni):
                peer_copy(d, k).wait_send()
                peer_copy(d, k).wait_recv()

    if dense:
        def apply(col):
            count = nz * tok_rows
            block = tok[col].reshape(count, tok.shape[-1])
            gate_value = jnp.dot(block, w_gate[0], preferred_element_type=F32)
            up_value = jnp.dot(block, w_up[0], preferred_element_type=F32)
            hidden = gate_value / (1.0 + jnp.exp(-gate_value)) * up_value
            row = lax.broadcasted_iota(jnp.int32, (tok_rows, fac.shape[-1]), 0)
            column = lax.broadcasted_iota(jnp.int32, (tok_rows, fac.shape[-1]), 1)
            weights = []
            for b in range(nz):
                line_of = fac[col, b, pl.ds(z * nx + x, 1), :]
                weights.append(jnp.sum(jnp.where(row == column, line_of, 0.0), axis=1, keepdims=True))
            hidden = (hidden * jnp.concatenate(weights, axis=0)).astype(BF16)
            return jnp.dot(hidden, w_down[0], preferred_element_type=F32).reshape(nz, tok_rows, -1)

        def res_copy(d):
            return remote(res.at[d - 1], xres.at[d - 1], rxs.at[d - 1], rxr.at[d - 1], node=lax.rem(x + nx - d, nx))

        def rup_copy(b):
            return remote(rup.at[b], rup.at[b], rus.at[b], rur.at[b], expert=above)

        def rdn_copy(b):
            return remote(rdn.at[b], rdn.at[b], rds.at[b], rdr.at[b], expert=below)

        def sum_step(s, carry):
            iu, id_ = s - z, s - (nz - 1 - z)
            bu, bd = nz - 1 - iu, id_

            @pl.when((iu >= 0) & (bu > z))
            def _():
                @pl.when(z == 0)
                def _():
                    rup[bu] = acc[bu].astype(BF16)

                @pl.when(z > 0)
                def _():
                    rup_copy(bu).wait_recv()
                    rup[bu] = (acc[bu] + rup[bu].astype(F32)).astype(BF16)

                rup_copy(bu).start()

            @pl.when((id_ >= 0) & (bd < z))
            def _():
                @pl.when(z == nz - 1)
                def _():
                    rdn[bd] = acc[bd].astype(BF16)

                @pl.when(z < nz - 1)
                def _():
                    rdn_copy(bd).wait_recv()
                    rdn[bd] = (acc[bd] + rdn[bd].astype(F32)).astype(BF16)

                rdn_copy(bd).start()

            return carry

        def finish_sum():
            @pl.when(z > 0)
            def _():
                rup_copy(z).wait_recv()
                acc[z] = acc[z] + rup[z].astype(F32)

            @pl.when(z < nz - 1)
            def _():
                rdn_copy(z).wait_recv()
                acc[z] = acc[z] + rdn[z].astype(F32)

            moe_out[...] = acc[z].astype(BF16)

        def drain_moe():
            def sends(b, carry):
                @pl.when((b <= z) & (z < nz - 1))
                def _():
                    for c in tok_up(b):
                        c.wait_send()

                @pl.when((b >= z) & (z > 0))
                def _():
                    for c in tok_dn(b):
                        c.wait_send()

                for d in range(1, nx):
                    for c in tok_x(d, b, x):
                        c.wait_send()

                @pl.when(b > z)
                def _():
                    rup_copy(b).wait_send()

                @pl.when(b < z)
                def _():
                    rdn_copy(b).wait_send()

                return carry

            lax.fori_loop(0, nz, sends, 0)
            for d in range(1, nx):
                res_copy(d).wait_send()

        lax.fori_loop(0, 1, tok_step, 0)
        start_first()
        lax.fori_loop(1, nz, tok_step, 0)
        acc[...] = apply(x)
        for d in range(1, nx):
            col = lax.rem(x + nx - d, nx)
            for b in range(nz):
                for c in tok_x(d, b, col):
                    c.wait_recv()
            res[d - 1] = apply(col).astype(BF16)
            res_copy(d).start()
    else:
        start_first()

    for copy in meta_copies:
        copy.wait_recv()
    for k in range(KINDS):
        for d in range(1, nx):
            first(d, k).wait_recv()
    hot_loop()
    if dense:
        for d in range(1, nx):
            res_copy(d).wait_recv()
            acc[...] = acc[...] + xres[d - 1].astype(F32)
        lax.fori_loop(0, 2 * nz - 2, sum_step, 0)
        finish_sum()
        drain_moe()
    finish_hot()
    drain()


def shards(
    tokens,
    slot_choice,
    gate_fixed,
    expert_gate,
    expert_up,
    expert_down,
    next_weights,
    hot_expert,
    slot_take,
):
    sizes = tuple(lax.axis_size(a) for a in ("groups", "expert", "node", "inner"))
    ng, nz, nx, ni = sizes
    tok_rows, width = tokens.shape
    _, kinds, half, hidden = next_weights.shape
    assert kinds == KINDS and hot_expert.shape[0] == 2
    experts = nz * nx
    dense = experts * ni <= 2 * slot_choice.shape[1]
    part = half // (nx * ng)
    items = KINDS * (1 + ng)
    vmem, smem = (pl.BlockSpec(memory_space=s) for s in (pltpu.VMEM, pltpu.SMEM))
    dma = pltpu.SemaphoreType.DMA
    operands, specs = [next_weights, hot_expert, slot_take], [vmem, smem, smem]
    outs = [jax.ShapeDtypeStruct((1, KINDS, ni * half, hidden), BF16)]
    out_specs = [pl.BlockSpec(memory_space=pl.ANY)]
    dx, dg, di = max(nx - 1, 1), max(ng - 1, 1), max(ni - 1, 1)
    scratch = [
        pltpu.VMEM((8, 128), jnp.int32),
        pltpu.VMEM((dg, 8, 128), jnp.int32),
        pltpu.VMEM((di, 8, 128), jnp.int32),
        pltpu.VMEM((dx, KINDS, part, hidden), BF16),
        pltpu.VMEM((items, part, hidden), BF16),
        pltpu.VMEM((items, part, hidden), BF16),
        pltpu.VMEM((1 + ng, KINDS, nx, ng, part, hidden), BF16),
        pltpu.VMEM((KINDS, half, hidden), BF16),
        pltpu.VMEM((di, KINDS, half, hidden), BF16),
        dma((dg + di,)), dma((dg + di,)),
        dma((dx, KINDS)), dma((dx, KINDS)),
        dma((items,)), dma((items,)),
        dma((items,)), dma((items,)),
        dma((dx, items)), dma((dx, items)),
        dma((dg, items, nx)), dma((dg, items, nx)),
        dma((KINDS,)),
        dma((di, KINDS)), dma((di, KINDS)),
    ]
    if dense:
        owner = slot_choice // ni
        share = gate_fixed.astype(F32) * (1.0 / 65536.0)
        tall, wide = -(-experts // 8) * 8, -(-tok_rows // 128) * 128
        named = owner[None] == jnp.arange(tall, dtype=jnp.int32)[:, None, None]
        factors = jnp.sum(jnp.where(named, share[None], 0.0), axis=2)
        factors = jnp.pad(factors, ((0, 0), (0, wide - tok_rows)))
        operands += [tokens, factors, expert_gate, expert_up, expert_down]
        specs += [vmem] * 5
        outs = [jax.ShapeDtypeStruct((tok_rows, width), BF16)] + outs
        out_specs = [vmem] + out_specs
        scratch += [
            pltpu.VMEM((nx, nz, tok_rows, width), BF16),
            pltpu.VMEM((nx, nz, tall, wide), F32),
            pltpu.VMEM((nz, tok_rows, width), F32),
            pltpu.VMEM((dx, nz, tok_rows, width), BF16),
            pltpu.VMEM((dx, nz, tok_rows, width), BF16),
            pltpu.VMEM((nz, tok_rows, width), BF16),
            pltpu.VMEM((nz, tok_rows, width), BF16),
            dma((nz,)), dma((nz,)), dma((nz,)), dma((nz,)), dma((dx, nz)), dma((dx, nz)),
            dma((nz,)), dma((nz,)), dma((nz,)), dma((nz,)), dma((dx, nz)), dma((dx, nz)),
            dma((dx,)), dma((dx,)),
            dma((nz,)), dma((nz,)), dma((nz,)), dma((nz,)),
        ]
    results = pl.pallas_call(
        functools.partial(kernel, sizes, dense),
        out_shape=outs,
        in_specs=specs,
        out_specs=out_specs,
        scratch_shapes=scratch,
        compiler_params=pltpu.CompilerParams(
            collective_id=0, has_side_effects=True, vmem_limit_bytes=56 * 2**20
        ),
    )(*operands)
    if dense:
        return tuple(results)
    moe_out = routed(tokens, slot_choice, gate_fixed, expert_gate, expert_up, expert_down)
    return moe_out, results[0]


def solution(mesh):
    tokens_spec = P(("groups", "expert", "node", "inner"), None)
    weights_spec = P(("expert", "node"), None, None)
    return jax.shard_map(
        shards,
        mesh=mesh,
        in_specs=(
            tokens_spec,
            tokens_spec,
            tokens_spec,
            weights_spec,
            weights_spec,
            weights_spec,
            P(("expert", "node"), None, "inner", None),
            P("groups"),
            P(("groups", "expert", "node", "inner")),
        ),
        out_specs=(tokens_spec, P(("groups", "expert", "node", "inner"), None, None, None)),
        check_vma=False,
    )
```

```python
import functools

import jax
import jax.numpy as jnp
from jax import lax
from jax.experimental import pallas as pl
from jax.experimental.pallas import tpu as pltpu
from jax.sharding import PartitionSpec as P

MESH = pl.DeviceIdType.MESH
BF16 = jnp.bfloat16
F32 = jnp.float32
KINDS = 3


def routed(tokens, slot_choice, gate_fixed, expert_gate, expert_up, expert_down):
    slot_count = lax.axis_size(("expert", "node", "inner"))
    tok_rows, model_width = tokens.shape
    pick_count = slot_choice.shape[1]
    capacity = max(2, 2 * tok_rows * pick_count // slot_count)
    flat_slot = slot_choice.reshape(-1)
    columns = jnp.arange(slot_count, dtype=jnp.int32)
    onehot = (flat_slot[:, None] == columns[None, :]).astype(jnp.int32)
    before = jnp.cumsum(onehot, axis=0) - onehot
    position = jnp.sum(before * onehot, axis=1)
    target = flat_slot * capacity + position
    source_rows = jnp.repeat(tokens, pick_count, axis=0)
    outgoing = jnp.zeros((slot_count * capacity, model_width), BF16).at[target].set(source_rows)
    outgoing = outgoing.reshape(slot_count, capacity, model_width)
    axes = ("expert", "node", "inner")
    block_rows = lax.all_to_all(outgoing, axes, split_axis=0, concat_axis=0, tiled=True)
    flat_rows = block_rows.reshape(-1, model_width)
    gate_value = jnp.dot(flat_rows, expert_gate[0], preferred_element_type=F32)
    up_value = jnp.dot(flat_rows, expert_up[0], preferred_element_type=F32)
    hidden = (jax.nn.silu(gate_value) * up_value).astype(BF16)
    result = jnp.dot(hidden, expert_down[0], preferred_element_type=F32).astype(BF16)
    returned = lax.all_to_all(
        result.reshape(block_rows.shape), axes, split_axis=0, concat_axis=0, tiled=True
    )
    back_rows = returned.reshape(slot_count * capacity, model_width)[target]
    factors = gate_fixed.reshape(-1).astype(F32) * (1.0 / 65536.0)
    weighted = back_rows.astype(F32) * factors[:, None]
    return jnp.sum(weighted.reshape(tok_rows, pick_count, model_width), axis=1).astype(BF16)


def pick(condition, yes, no):
    return lax.select_n(condition, no, yes)


def kernel(sizes, dense, *refs):
    ng, nz, nx, ni = sizes
    refs = list(refs)
    nw, hot, take = refs[:3]
    del refs[:3]
    if dense:
        tokens, factors, *w_in = refs[:5]
        del refs[:5]
        moe_out = refs.pop(0)
    out = refs.pop(0)
    (meta, meta_y, meta_i, xin, up, dn, full, own_out, peer_out) = refs[:9]
    del refs[:9]
    (m_send, m_recv, s1s, s1r, ups, upr, dns, dnr, xs, xr, ys, yr, os, ps, pr) = refs[:15]
    del refs[:15]

    g, z, x, i = (lax.axis_index(a) for a in ("groups", "expert", "node", "inner"))
    half = nw.shape[2]
    part = half // (nx * ng)
    experts = nz * nx
    unions = 1 + ng
    items = KINDS * unions
    above, below = lax.rem(z + 1, nz), lax.rem(z + nz - 1, nz)

    def rows(p, q):
        return pl.ds(pl.multiple_of((p * ng + q) * part, part), part)

    def remote(src, dst, send, recv, **where):
        return pltpu.make_async_remote_copy(
            src_ref=src, dst_ref=dst, send_sem=send, recv_sem=recv, device_id=where, device_id_type=MESH
        )

    barrier = pltpu.get_barrier_semaphore()

    def greet(**where):
        pl.semaphore_signal(barrier, inc=1, device_id=where, device_id_type=MESH)

    for d in range(1, nx):
        greet(node=lax.rem(x + d, nx))
    for d in range(1, ng):
        greet(groups=lax.rem(g + d, ng))
    for d in range(1, ni):
        greet(inner=lax.rem(i + d, ni))

    @pl.when(z > 0)
    def _():
        greet(expert=below)

    @pl.when(z < nz - 1)
    def _():
        greet(expert=above)

    ends = (z > 0).astype(jnp.int32) + (z < nz - 1).astype(jnp.int32)
    pl.semaphore_wait(barrier, nx - 1 + ng - 1 + ni - 1 + ends)

    last = experts - 1
    other = hot[0] + hot[1] - last
    last_place = pick(hot[0] == last, jnp.int32(0), jnp.int32(1))
    code = pick(take[0] == 2, jnp.int32(2), pick(take[0] == last_place, jnp.int32(0), jnp.int32(1)))
    line = lax.broadcasted_iota(jnp.int32, meta.shape, 0)
    meta[...] = jnp.where(line == 0, other, code)
    meta_copies = []
    for d in range(1, ng):
        n = len(meta_copies)
        meta_copies.append(
            remote(meta, meta_y.at[d - 1], m_send.at[n], m_recv.at[n], groups=lax.rem(g + d, ng))
        )
    for d in range(1, ni):
        n = len(meta_copies)
        meta_copies.append(
            remote(meta, meta_i.at[d - 1], m_send.at[n], m_recv.at[n], inner=lax.rem(i + d, ni))
        )
    for copy in meta_copies:
        copy.start()

    if dense:
        (w_gate, w_up, w_down, w_sem) = refs[:4]
        del refs[:4]
        load_copies = [
            pltpu.make_async_copy(src, dst, w_sem.at[n])
            for n, (src, dst) in enumerate(zip(w_in, (w_gate, w_up, w_down)))
        ]
        for copy in load_copies:
            copy.start()
        (tok, fac, acc, res, xres, rup, rdn) = refs[:7]
        (tus, tur, tds, tdr, txs, txr, fus, fur, fds, fdr, fxs, fxr, rxs, rxr, rus, rur, rds, rdr) = refs[7:]
        tok_rows = tokens.shape[0]

        def tok_up(b):
            return [
                remote(tok.at[x, b], tok.at[x, b], tus.at[b], tur.at[b], expert=above),
                remote(fac.at[x, b], fac.at[x, b], fus.at[b], fur.at[b], expert=above),
            ]

        def tok_dn(b):
            return [
                remote(tok.at[x, b], tok.at[x, b], tds.at[b], tdr.at[b], expert=below),
                remote(fac.at[x, b], fac.at[x, b], fds.at[b], fdr.at[b], expert=below),
            ]

        def tok_x(d, b, col):
            to = lax.rem(x + d, nx)
            return [
                remote(tok.at[col, b], tok.at[col, b], txs.at[d - 1, b], txr.at[d - 1, b], node=to),
                remote(fac.at[col, b], fac.at[col, b], fxs.at[d - 1, b], fxr.at[d - 1, b], node=to),
            ]

        tok[x, z] = tokens[...]
        fac[x, z] = factors[...]

        def tok_step(s, carry):
            bu, bd = z - s, z + s

            @pl.when(bu >= 0)
            def _():
                @pl.when(s > 0)
                def _():
                    for c in tok_up(bu):
                        c.wait_recv()

                @pl.when(z < nz - 1)
                def _():
                    for c in tok_up(bu):
                        c.start()

                for d in range(1, nx):
                    for c in tok_x(d, bu, x):
                        c.start()

            @pl.when(bd < nz)
            def _():
                @pl.when(s > 0)
                def _():
                    for c in tok_dn(bd):
                        c.wait_recv()

                @pl.when(z > 0)
                def _():
                    for c in tok_dn(bd):
                        c.start()

                @pl.when(s > 0)
                def _():
                    for d in range(1, nx):
                        for c in tok_x(d, bd, x):
                            c.start()

            return carry

    def first(d, k):
        to = lax.rem(x + d, nx)
        return remote(nw.at[0, k, rows(to, g)], xin.at[d - 1, k], s1s.at[d - 1, k], s1r.at[d - 1, k], node=to)

    def start_first():
        for k in range(KINDS):
            for d in range(1, nx):
                first(d, k).start()

    def up_copy(j):
        return remote(up.at[j], up.at[j], ups.at[j], upr.at[j], expert=above)

    def dn_copy(j):
        return remote(dn.at[j], dn.at[j], dns.at[j], dnr.at[j], expert=below)

    def x_copy(d, j, p):
        k, u = j // unions, j % unions
        spot = full.at[u, k, p, g]
        return remote(spot, spot, xs.at[d - 1, j], xr.at[d - 1, j], node=lax.rem(x + d, nx))

    def y_copy(d, j, p, q):
        k, u = j // unions, j % unions
        spot = full.at[u, k, p, q]
        return remote(spot, spot, ys.at[d - 1, j, p], yr.at[d - 1, j, p], groups=lax.rem(g + d, ng))

    def y_wanted(d, j):
        u = j % unions
        return (u == 0) | (u == 1 + lax.rem(g + d, ng))

    def y_start(j, p):
        for d in range(1, ng):
            @pl.when(y_wanted(d, j))
            def _():
                y_copy(d, j, p, g).start()

    def hot_steps():
        others = [other] + [jnp.max(meta_y[d - 1, 0:1, :]) for d in range(1, ng)]

        def owner(u):
            expert = jnp.int32(last)
            for d in range(ng):
                expert = pick(u == 1 + lax.rem(g + ng - d, ng), others[d], expert)
            return expert // nx, expert % nx

        def here(j):
            k, u = j // unions, j % unions
            oz, ox = owner(u)
            value = nw[0, k, rows(x, g), :]
            for d in range(1, nx):
                value = pick(ox == lax.rem(x + nx - d, nx), xin[d - 1, k], value)
            return oz, value

        def line_step(j, buffer, copy, first_one, last_one):
            @pl.when((j >= 0) & (j < items))
            def _():
                oz, value = here(j)

                @pl.when(first_one)
                def _():
                    buffer[j] = value

                @pl.when(jnp.logical_not(first_one))
                def _():
                    copy(j).wait_recv()
                    buffer[j] = pick(oz == z, value, buffer[j])

                @pl.when(jnp.logical_not(last_one))
                def _():
                    copy(j).start()

        lag = 2
        far, near = jnp.maximum(z, nz - 1 - z), jnp.minimum(z, nz - 1 - z)

        def step(s, carry):
            j1 = s - near

            @pl.when((j1 >= 0) & (j1 < items) & (j1 % unions == 0))
            def _():
                for d in range(1, nx):
                    first(d, j1 // unions).wait_recv()

            line_step(s - z, up, up_copy, z == 0, z == nz - 1)
            line_step(s - (nz - 1 - z), dn, dn_copy, z == nz - 1, z == 0)
            j = s - far

            @pl.when((j >= 0) & (j < items))
            def _():
                k, u = j // unions, j % unions
                oz, _ = owner(u)
                full[u, k, x, g] = pick(oz <= z, up[j], dn[j])
                for d in range(1, nx):
                    x_copy(d, j, x).start()
                y_start(j, x)

            j2 = j - lag

            @pl.when((j2 >= 0) & (j2 < items))
            def _():
                for d in range(1, nx):
                    p = lax.rem(x + nx - d, nx)
                    x_copy(d, j2, p).wait_recv()
                    y_start(j2, p)

            return carry

        return step, items + nz - 1 + lag

    def out_rows():
        return pl.ds(pl.multiple_of(i * half, half), half)

    def own_copy(k):
        return pltpu.make_async_copy(own_out.at[k], out.at[0, k, out_rows()], os.at[k])

    def peer_copy(d, k):
        to = lax.rem(i + d, ni)
        return remote(peer_out.at[d - 1, k], out.at[0, k, out_rows()], ps.at[d - 1, k], pr.at[d - 1, k], inner=to)

    def finish_hot():
        codes = [jnp.max(meta_i[d - 1, 1:2, :]) for d in range(1, ni)]
        for k in range(KINDS):
            for d in range(1, ng):
                q = lax.rem(g + ng - d, ng)
                for p in range(nx):
                    y_copy(d, k * unions, p, q).wait_recv()
                    y_copy(d, k * unions + 1 + g, p, q).wait_recv()
            known = full[0, k].reshape(half, full.shape[-1])
            second = full[1 + g, k].reshape(half, full.shape[-1])

            def chosen(c):
                return pick(c == 2, jnp.zeros_like(known), pick(c == 0, known, second))

            for d in range(1, ni):
                peer_out[d - 1, k] = chosen(codes[ni - d - 1])
                peer_copy(d, k).start()
            own_out[k] = chosen(code)
            own_copy(k).start()

    def drain():
        for copy in meta_copies:
            copy.wait_send()
        for k in range(KINDS):
            for d in range(1, nx):
                first(d, k).wait_send()

        def sends(j, carry):
            @pl.when(z < nz - 1)
            def _():
                up_copy(j).wait_send()

            @pl.when(z > 0)
            def _():
                dn_copy(j).wait_send()

            for d in range(1, nx):
                x_copy(d, j, x).wait_send()
            for d in range(1, ng):
                @pl.when(y_wanted(d, j))
                def _():
                    for p in range(nx):
                        y_copy(d, j, p, g).wait_send()
            return carry

        lax.fori_loop(0, items, sends, 0)
        for k in range(KINDS):
            own_copy(k).wait()
            for d in range(1, ni):
                peer_copy(d, k).wait_send()
                peer_copy(d, k).wait_recv()

    if dense:
        def apply(col):
            count = nz * tok_rows
            block = tok[col].reshape(count, tok.shape[-1])
            gate_value = jnp.dot(block, w_gate[0], preferred_element_type=F32)
            up_value = jnp.dot(block, w_up[0], preferred_element_type=F32)
            hidden = gate_value / (1.0 + jnp.exp(-gate_value)) * up_value
            row = lax.broadcasted_iota(jnp.int32, (tok_rows, fac.shape[-1]), 0)
            column = lax.broadcasted_iota(jnp.int32, (tok_rows, fac.shape[-1]), 1)
            weights = []
            for b in range(nz):
                line_of = fac[col, b, pl.ds(z * nx + x, 1), :]
                weights.append(jnp.sum(jnp.where(row == column, line_of, 0.0), axis=1, keepdims=True))
            hidden = (hidden * jnp.concatenate(weights, axis=0)).astype(BF16)
            return jnp.dot(hidden, w_down[0], preferred_element_type=F32).reshape(nz, tok_rows, -1)

        def res_copy(d):
            return remote(res.at[d - 1], xres.at[d - 1], rxs.at[d - 1], rxr.at[d - 1], node=lax.rem(x + nx - d, nx))

        def rup_copy(b):
            return remote(rup.at[b], rup.at[b], rus.at[b], rur.at[b], expert=above)

        def rdn_copy(b):
            return remote(rdn.at[b], rdn.at[b], rds.at[b], rdr.at[b], expert=below)

        def sum_step(s, carry):
            iu, id_ = s - z, s - (nz - 1 - z)
            bu, bd = nz - 1 - iu, id_

            @pl.when((iu >= 0) & (bu > z))
            def _():
                @pl.when(z == 0)
                def _():
                    rup[bu] = acc[bu].astype(BF16)

                @pl.when(z > 0)
                def _():
                    rup_copy(bu).wait_recv()
                    rup[bu] = (acc[bu] + rup[bu].astype(F32)).astype(BF16)

                rup_copy(bu).start()

            @pl.when((id_ >= 0) & (bd < z))
            def _():
                @pl.when(z == nz - 1)
                def _():
                    rdn[bd] = acc[bd].astype(BF16)

                @pl.when(z < nz - 1)
                def _():
                    rdn_copy(bd).wait_recv()
                    rdn[bd] = (acc[bd] + rdn[bd].astype(F32)).astype(BF16)

                rdn_copy(bd).start()

            return carry

        def finish_sum():
            @pl.when(z > 0)
            def _():
                rup_copy(z).wait_recv()
                acc[z] = acc[z] + rup[z].astype(F32)

            @pl.when(z < nz - 1)
            def _():
                rdn_copy(z).wait_recv()
                acc[z] = acc[z] + rdn[z].astype(F32)

            moe_out[...] = acc[z].astype(BF16)

        def drain_moe():
            def sends(b, carry):
                @pl.when((b <= z) & (z < nz - 1))
                def _():
                    for c in tok_up(b):
                        c.wait_send()

                @pl.when((b >= z) & (z > 0))
                def _():
                    for c in tok_dn(b):
                        c.wait_send()

                for d in range(1, nx):
                    for c in tok_x(d, b, x):
                        c.wait_send()

                @pl.when(b > z)
                def _():
                    rup_copy(b).wait_send()

                @pl.when(b < z)
                def _():
                    rdn_copy(b).wait_send()

                return carry

            lax.fori_loop(0, nz, sends, 0)
            for d in range(1, nx):
                res_copy(d).wait_send()

        start_first()
        lax.fori_loop(0, nz, tok_step, 0)
    else:
        start_first()
    for copy in meta_copies:
        copy.wait_recv()
    hot_step, hot_count = hot_steps()
    if dense:
        at_own, at_other, at_sum = (hot_count * n // 14 for n in (2, 5, 10))
        lax.fori_loop(0, at_own, hot_step, 0)
        for copy in load_copies:
            copy.wait()
        acc[...] = apply(x)
        lax.fori_loop(at_own, at_other, hot_step, 0)
        for d in range(1, nx):
            col = lax.rem(x + nx - d, nx)
            for b in range(nz):
                for c in tok_x(d, b, col):
                    c.wait_recv()
            res[d - 1] = apply(col).astype(BF16)
            res_copy(d).start()
        lax.fori_loop(at_other, at_sum, hot_step, 0)
        for d in range(1, nx):
            res_copy(d).wait_recv()
            acc[...] = acc[...] + xres[d - 1].astype(F32)

        def both(s, carry):
            hot_step(s, carry)
            return sum_step(s - at_sum, carry)

        lax.fori_loop(at_sum, hot_count, both, 0)
        lax.fori_loop(hot_count - at_sum, 2 * nz - 2, sum_step, 0)
        finish_hot()
        finish_sum()
        drain_moe()
    else:
        lax.fori_loop(0, hot_count, hot_step, 0)
        finish_hot()
    drain()


def shards(
    tokens,
    slot_choice,
    gate_fixed,
    expert_gate,
    expert_up,
    expert_down,
    next_weights,
    hot_expert,
    slot_take,
):
    sizes = tuple(lax.axis_size(a) for a in ("groups", "expert", "node", "inner"))
    ng, nz, nx, ni = sizes
    tok_rows, width = tokens.shape
    _, kinds, half, hidden = next_weights.shape
    assert kinds == KINDS and hot_expert.shape[0] == 2
    experts = nz * nx
    dense = experts * ni <= 2 * slot_choice.shape[1]
    part = half // (nx * ng)
    items = KINDS * (1 + ng)
    vmem, smem = (pl.BlockSpec(memory_space=s) for s in (pltpu.VMEM, pltpu.SMEM))
    dma = pltpu.SemaphoreType.DMA
    operands, specs = [next_weights, hot_expert, slot_take], [vmem, smem, smem]
    outs = [jax.ShapeDtypeStruct((1, KINDS, ni * half, hidden), BF16)]
    out_specs = [pl.BlockSpec(memory_space=pl.ANY)]
    dx, dg, di = max(nx - 1, 1), max(ng - 1, 1), max(ni - 1, 1)
    scratch = [
        pltpu.VMEM((8, 128), jnp.int32),
        pltpu.VMEM((dg, 8, 128), jnp.int32),
        pltpu.VMEM((di, 8, 128), jnp.int32),
        pltpu.VMEM((dx, KINDS, part, hidden), BF16),
        pltpu.VMEM((items, part, hidden), BF16),
        pltpu.VMEM((items, part, hidden), BF16),
        pltpu.VMEM((1 + ng, KINDS, nx, ng, part, hidden), BF16),
        pltpu.VMEM((KINDS, half, hidden), BF16),
        pltpu.VMEM((di, KINDS, half, hidden), BF16),
        dma((dg + di,)), dma((dg + di,)),
        dma((dx, KINDS)), dma((dx, KINDS)),
        dma((items,)), dma((items,)),
        dma((items,)), dma((items,)),
        dma((dx, items)), dma((dx, items)),
        dma((dg, items, nx)), dma((dg, items, nx)),
        dma((KINDS,)),
        dma((di, KINDS)), dma((di, KINDS)),
    ]
    if dense:
        owner = slot_choice // ni
        share = gate_fixed.astype(F32) * (1.0 / 65536.0)
        tall, wide = -(-experts // 8) * 8, -(-tok_rows // 128) * 128
        named = owner[None] == jnp.arange(tall, dtype=jnp.int32)[:, None, None]
        factors = jnp.sum(jnp.where(named, share[None], 0.0), axis=2)
        factors = jnp.pad(factors, ((0, 0), (0, wide - tok_rows)))
        operands += [tokens, factors, expert_gate, expert_up, expert_down]
        specs += [vmem] * 2 + [pl.BlockSpec(memory_space=pl.ANY)] * 3
        outs = [jax.ShapeDtypeStruct((tok_rows, width), BF16)] + outs
        out_specs = [vmem] + out_specs
        scratch += [
            pltpu.VMEM(expert_gate.shape, BF16),
            pltpu.VMEM(expert_up.shape, BF16),
            pltpu.VMEM(expert_down.shape, BF16),
            dma((3,)),
            pltpu.VMEM((nx, nz, tok_rows, width), BF16),
            pltpu.VMEM((nx, nz, tall, wide), F32),
            pltpu.VMEM((nz, tok_rows, width), F32),
            pltpu.VMEM((dx, nz, tok_rows, width), BF16),
            pltpu.VMEM((dx, nz, tok_rows, width), BF16),
            pltpu.VMEM((nz, tok_rows, width), BF16),
            pltpu.VMEM((nz, tok_rows, width), BF16),
            dma((nz,)), dma((nz,)), dma((nz,)), dma((nz,)), dma((dx, nz)), dma((dx, nz)),
            dma((nz,)), dma((nz,)), dma((nz,)), dma((nz,)), dma((dx, nz)), dma((dx, nz)),
            dma((dx,)), dma((dx,)),
            dma((nz,)), dma((nz,)), dma((nz,)), dma((nz,)),
        ]
    results = pl.pallas_call(
        functools.partial(kernel, sizes, dense),
        out_shape=outs,
        in_specs=specs,
        out_specs=out_specs,
        scratch_shapes=scratch,
        compiler_params=pltpu.CompilerParams(
            collective_id=0, has_side_effects=True, vmem_limit_bytes=56 * 2**20
        ),
    )(*operands)
    if dense:
        return tuple(results)
    moe_out = routed(tokens, slot_choice, gate_fixed, expert_gate, expert_up, expert_down)
    return moe_out, results[0]


def solution(mesh):
    tokens_spec = P(("groups", "expert", "node", "inner"), None)
    weights_spec = P(("expert", "node"), None, None)
    return jax.shard_map(
        shards,
        mesh=mesh,
        in_specs=(
            tokens_spec,
            tokens_spec,
            tokens_spec,
            weights_spec,
            weights_spec,
            weights_spec,
            P(("expert", "node"), None, "inner", None),
            P("groups"),
            P(("groups", "expert", "node", "inner")),
        ),
        out_specs=(tokens_spec, P(("groups", "expert", "node", "inner"), None, None, None)),
        check_vma=False,
    )
```

```python
import functools

import jax
import jax.numpy as jnp
from jax import lax
from jax.experimental import pallas as pl
from jax.experimental.pallas import tpu as pltpu
from jax.sharding import PartitionSpec as P

MESH = pl.DeviceIdType.MESH
BF16 = jnp.bfloat16
F32 = jnp.float32
KINDS = 3


def routed(tokens, slot_choice, gate_fixed, expert_gate, expert_up, expert_down):
    slot_count = lax.axis_size(("expert", "node", "inner"))
    tok_rows, model_width = tokens.shape
    pick_count = slot_choice.shape[1]
    capacity = max(2, 2 * tok_rows * pick_count // slot_count)
    flat_slot = slot_choice.reshape(-1)
    columns = jnp.arange(slot_count, dtype=jnp.int32)
    onehot = (flat_slot[:, None] == columns[None, :]).astype(jnp.int32)
    before = jnp.cumsum(onehot, axis=0) - onehot
    position = jnp.sum(before * onehot, axis=1)
    target = flat_slot * capacity + position
    source_rows = jnp.repeat(tokens, pick_count, axis=0)
    outgoing = jnp.zeros((slot_count * capacity, model_width), BF16).at[target].set(source_rows)
    outgoing = outgoing.reshape(slot_count, capacity, model_width)
    axes = ("expert", "node", "inner")
    block_rows = lax.all_to_all(outgoing, axes, split_axis=0, concat_axis=0, tiled=True)
    flat_rows = block_rows.reshape(-1, model_width)
    gate_value = jnp.dot(flat_rows, expert_gate[0], preferred_element_type=F32)
    up_value = jnp.dot(flat_rows, expert_up[0], preferred_element_type=F32)
    hidden = (jax.nn.silu(gate_value) * up_value).astype(BF16)
    result = jnp.dot(hidden, expert_down[0], preferred_element_type=F32).astype(BF16)
    returned = lax.all_to_all(
        result.reshape(block_rows.shape), axes, split_axis=0, concat_axis=0, tiled=True
    )
    back_rows = returned.reshape(slot_count * capacity, model_width)[target]
    factors = gate_fixed.reshape(-1).astype(F32) * (1.0 / 65536.0)
    weighted = back_rows.astype(F32) * factors[:, None]
    return jnp.sum(weighted.reshape(tok_rows, pick_count, model_width), axis=1).astype(BF16)


def pick(condition, yes, no):
    return lax.select_n(condition, no, yes)


def kernel(sizes, dense, *refs):
    ng, nz, nx, ni = sizes
    refs = list(refs)
    nw, hot, take = refs[:3]
    del refs[:3]
    if dense:
        tokens, factors, *w_in = refs[:5]
        del refs[:5]
        moe_out = refs.pop(0)
    out = refs.pop(0)
    (meta, meta_y, meta_i, xin, up, dn, full, own_out, peer_out) = refs[:9]
    del refs[:9]
    (m_send, m_recv, s1s, s1r, ups, upr, dns, dnr, xs, xr, ys, yr, os, ps, pr) = refs[:15]
    del refs[:15]

    g, z, x, i = (lax.axis_index(a) for a in ("groups", "expert", "node", "inner"))
    half = nw.shape[2]
    part = half // (nx * ng)
    experts = nz * nx
    unions = 1 + ng
    items = KINDS * unions
    above, below = lax.rem(z + 1, nz), lax.rem(z + nz - 1, nz)

    def rows(p, q):
        return pl.ds(pl.multiple_of((p * ng + q) * part, part), part)

    def remote(src, dst, send, recv, **where):
        return pltpu.make_async_remote_copy(
            src_ref=src, dst_ref=dst, send_sem=send, recv_sem=recv, device_id=where, device_id_type=MESH
        )

    barrier = pltpu.get_barrier_semaphore()

    def greet(**where):
        pl.semaphore_signal(barrier, inc=1, device_id=where, device_id_type=MESH)

    for d in range(1, nx):
        greet(node=lax.rem(x + d, nx))
    for d in range(1, ng):
        greet(groups=lax.rem(g + d, ng))
    for d in range(1, ni):
        greet(inner=lax.rem(i + d, ni))

    @pl.when(z > 0)
    def _():
        greet(expert=below)

    @pl.when(z < nz - 1)
    def _():
        greet(expert=above)

    ends = (z > 0).astype(jnp.int32) + (z < nz - 1).astype(jnp.int32)
    pl.semaphore_wait(barrier, nx - 1 + ng - 1 + ni - 1 + ends)

    last = experts - 1
    other = hot[0] + hot[1] - last
    last_place = pick(hot[0] == last, jnp.int32(0), jnp.int32(1))
    code = pick(take[0] == 2, jnp.int32(2), pick(take[0] == last_place, jnp.int32(0), jnp.int32(1)))
    line = lax.broadcasted_iota(jnp.int32, meta.shape, 0)
    meta[...] = jnp.where(line == 0, other, code)
    meta_copies = []
    for d in range(1, ng):
        n = len(meta_copies)
        meta_copies.append(
            remote(meta, meta_y.at[d - 1], m_send.at[n], m_recv.at[n], groups=lax.rem(g + d, ng))
        )
    for d in range(1, ni):
        n = len(meta_copies)
        meta_copies.append(
            remote(meta, meta_i.at[d - 1], m_send.at[n], m_recv.at[n], inner=lax.rem(i + d, ni))
        )
    for copy in meta_copies:
        copy.start()

    if dense:
        (w_gate, w_up, w_down, w_sem) = refs[:4]
        del refs[:4]
        load_copies = [
            pltpu.make_async_copy(src, dst, w_sem.at[n])
            for n, (src, dst) in enumerate(zip(w_in, (w_gate, w_up, w_down)))
        ]
        for copy in load_copies:
            copy.start()
        (tok, fac, acc, res, xres, rup, rdn) = refs[:7]
        (tus, tur, tds, tdr, txs, txr, fus, fur, fds, fdr, fxs, fxr, rxs, rxr, rus, rur, rds, rdr) = refs[7:]
        tok_rows = tokens.shape[0]

        def tok_up(b, d, col):
            return [
                remote(tok.at[col, b], tok.at[col, b], tus.at[b, d], tur.at[b, d], expert=above),
                remote(fac.at[col, b], fac.at[col, b], fus.at[b, d], fur.at[b, d], expert=above),
            ]

        def tok_dn(b, d, col):
            return [
                remote(tok.at[col, b], tok.at[col, b], tds.at[b, d], tdr.at[b, d], expert=below),
                remote(fac.at[col, b], fac.at[col, b], fds.at[b, d], fdr.at[b, d], expert=below),
            ]

        def tok_x(d, col):
            to = lax.rem(x + d, nx)
            return [
                remote(tok.at[col, z], tok.at[col, z], txs.at[d - 1], txr.at[d - 1], node=to),
                remote(fac.at[col, z], fac.at[col, z], fxs.at[d - 1], fxr.at[d - 1], node=to),
            ]

        tok[x, z] = tokens[...]
        fac[x, z] = factors[...]
        for d in range(1, nx):
            for c in tok_x(d, x):
                c.start()

        def tok_step(s, carry):
            bu, bd = z - s, z + s
            for d in range(nx):
                col = lax.rem(x + nx - d, nx)

                @pl.when(bu >= 0)
                def _():
                    @pl.when(s > 0)
                    def _():
                        for c in tok_up(bu, d, col):
                            c.wait_recv()

                    if d > 0:
                        @pl.when(s == 0)
                        def _():
                            for c in tok_x(d, col):
                                c.wait_recv()

                    @pl.when(z < nz - 1)
                    def _():
                        for c in tok_up(bu, d, col):
                            c.start()

                @pl.when(bd < nz)
                def _():
                    @pl.when(s > 0)
                    def _():
                        for c in tok_dn(bd, d, col):
                            c.wait_recv()

                    @pl.when(z > 0)
                    def _():
                        for c in tok_dn(bd, d, col):
                            c.start()

            return carry

    def first(d, k):
        to = lax.rem(x + d, nx)
        return remote(nw.at[0, k, rows(to, g)], xin.at[d - 1, k], s1s.at[d - 1, k], s1r.at[d - 1, k], node=to)

    def start_first():
        for k in range(KINDS):
            for d in range(1, nx):
                first(d, k).start()

    def up_copy(j):
        return remote(up.at[j], up.at[j], ups.at[j], upr.at[j], expert=above)

    def dn_copy(j):
        return remote(dn.at[j], dn.at[j], dns.at[j], dnr.at[j], expert=below)

    def x_copy(d, j, p):
        k, u = j // unions, j % unions
        spot = full.at[u, k, p, g]
        return remote(spot, spot, xs.at[d - 1, j], xr.at[d - 1, j], node=lax.rem(x + d, nx))

    def y_copy(d, j, p, q):
        k, u = j // unions, j % unions
        spot = full.at[u, k, p, q]
        return remote(spot, spot, ys.at[d - 1, j, p], yr.at[d - 1, j, p], groups=lax.rem(g + d, ng))

    def y_wanted(d, j):
        u = j % unions
        return (u == 0) | (u == 1 + lax.rem(g + d, ng))

    def y_start(j, p):
        for d in range(1, ng):
            @pl.when(y_wanted(d, j))
            def _():
                y_copy(d, j, p, g).start()

    def hot_steps():
        others = [other] + [jnp.max(meta_y[d - 1, 0:1, :]) for d in range(1, ng)]

        def owner(u):
            expert = jnp.int32(last)
            for d in range(ng):
                expert = pick(u == 1 + lax.rem(g + ng - d, ng), others[d], expert)
            return expert // nx, expert % nx

        def here(j):
            k, u = j // unions, j % unions
            oz, ox = owner(u)
            value = nw[0, k, rows(x, g), :]
            for d in range(1, nx):
                value = pick(ox == lax.rem(x + nx - d, nx), xin[d - 1, k], value)
            return oz, value

        def line_step(j, buffer, copy, first_one, last_one):
            @pl.when((j >= 0) & (j < items))
            def _():
                oz, value = here(j)

                @pl.when(first_one)
                def _():
                    buffer[j] = value

                @pl.when(jnp.logical_not(first_one))
                def _():
                    copy(j).wait_recv()
                    buffer[j] = pick(oz == z, value, buffer[j])

                @pl.when(jnp.logical_not(last_one))
                def _():
                    copy(j).start()

        lag = 2
        far, near = jnp.maximum(z, nz - 1 - z), jnp.minimum(z, nz - 1 - z)

        def step(s, carry):
            j1 = s - near

            @pl.when((j1 >= 0) & (j1 < items) & (j1 % unions == 0))
            def _():
                for d in range(1, nx):
                    first(d, j1 // unions).wait_recv()

            line_step(s - z, up, up_copy, z == 0, z == nz - 1)
            line_step(s - (nz - 1 - z), dn, dn_copy, z == nz - 1, z == 0)
            j = s - far

            @pl.when((j >= 0) & (j < items))
            def _():
                k, u = j // unions, j % unions
                oz, _ = owner(u)
                full[u, k, x, g] = pick(oz <= z, up[j], dn[j])
                for d in range(1, nx):
                    x_copy(d, j, x).start()
                y_start(j, x)

            j2 = j - lag

            @pl.when((j2 >= 0) & (j2 < items))
            def _():
                for d in range(1, nx):
                    p = lax.rem(x + nx - d, nx)
                    x_copy(d, j2, p).wait_recv()
                    y_start(j2, p)

            return carry

        return step, items + nz - 1 + lag

    def out_rows():
        return pl.ds(pl.multiple_of(i * half, half), half)

    def own_copy(k):
        return pltpu.make_async_copy(own_out.at[k], out.at[0, k, out_rows()], os.at[k])

    def peer_copy(d, k):
        to = lax.rem(i + d, ni)
        return remote(peer_out.at[d - 1, k], out.at[0, k, out_rows()], ps.at[d - 1, k], pr.at[d - 1, k], inner=to)

    def finish_hot(kinds):
        codes = [jnp.max(meta_i[d - 1, 1:2, :]) for d in range(1, ni)]
        for k in kinds:
            for d in range(1, ng):
                q = lax.rem(g + ng - d, ng)
                for p in range(nx):
                    y_copy(d, k * unions, p, q).wait_recv()
                    y_copy(d, k * unions + 1 + g, p, q).wait_recv()
            known = full[0, k].reshape(half, full.shape[-1])
            second = full[1 + g, k].reshape(half, full.shape[-1])

            def chosen(c):
                return pick(c == 2, jnp.zeros_like(known), pick(c == 0, known, second))

            for d in range(1, ni):
                peer_out[d - 1, k] = chosen(codes[ni - d - 1])
                peer_copy(d, k).start()
            own_out[k] = chosen(code)
            own_copy(k).start()

    def drain():
        for copy in meta_copies:
            copy.wait_send()
        for k in range(KINDS):
            for d in range(1, nx):
                first(d, k).wait_send()

        def sends(j, carry):
            @pl.when(z < nz - 1)
            def _():
                up_copy(j).wait_send()

            @pl.when(z > 0)
            def _():
                dn_copy(j).wait_send()

            for d in range(1, nx):
                x_copy(d, j, x).wait_send()
            for d in range(1, ng):
                @pl.when(y_wanted(d, j))
                def _():
                    for p in range(nx):
                        y_copy(d, j, p, g).wait_send()
            return carry

        lax.fori_loop(0, items, sends, 0)
        for k in range(KINDS):
            own_copy(k).wait()
            for d in range(1, ni):
                peer_copy(d, k).wait_send()
                peer_copy(d, k).wait_recv()

    if dense:
        def apply(col):
            count = nz * tok_rows
            block = tok[col].reshape(count, tok.shape[-1])
            gate_value = jnp.dot(block, w_gate[0], preferred_element_type=F32)
            up_value = jnp.dot(block, w_up[0], preferred_element_type=F32)
            hidden = gate_value / (1.0 + jnp.exp(-gate_value)) * up_value
            row = lax.broadcasted_iota(jnp.int32, (tok_rows, fac.shape[-1]), 0)
            column = lax.broadcasted_iota(jnp.int32, (tok_rows, fac.shape[-1]), 1)
            weights = []
            for b in range(nz):
                line_of = fac[col, b, pl.ds(z * nx + x, 1), :]
                weights.append(jnp.sum(jnp.where(row == column, line_of, 0.0), axis=1, keepdims=True))
            hidden = (hidden * jnp.concatenate(weights, axis=0)).astype(BF16)
            return jnp.dot(hidden, w_down[0], preferred_element_type=F32).reshape(nz, tok_rows, -1)

        def res_copy(d):
            return remote(res.at[d - 1], xres.at[d - 1], rxs.at[d - 1], rxr.at[d - 1], node=lax.rem(x + nx - d, nx))

        def rup_copy(b):
            return remote(rup.at[b], rup.at[b], rus.at[b], rur.at[b], expert=above)

        def rdn_copy(b):
            return remote(rdn.at[b], rdn.at[b], rds.at[b], rdr.at[b], expert=below)

        def sum_step(s, carry):
            iu, id_ = s - z, s - (nz - 1 - z)
            bu, bd = nz - 1 - iu, id_

            @pl.when((iu >= 0) & (bu > z))
            def _():
                @pl.when(z == 0)
                def _():
                    rup[bu] = acc[bu].astype(BF16)

                @pl.when(z > 0)
                def _():
                    rup_copy(bu).wait_recv()
                    rup[bu] = (acc[bu] + rup[bu].astype(F32)).astype(BF16)

                rup_copy(bu).start()

            @pl.when((id_ >= 0) & (bd < z))
            def _():
                @pl.when(z == nz - 1)
                def _():
                    rdn[bd] = acc[bd].astype(BF16)

                @pl.when(z < nz - 1)
                def _():
                    rdn_copy(bd).wait_recv()
                    rdn[bd] = (acc[bd] + rdn[bd].astype(F32)).astype(BF16)

                rdn_copy(bd).start()

            return carry

        def finish_sum():
            @pl.when(z > 0)
            def _():
                rup_copy(z).wait_recv()
                acc[z] = acc[z] + rup[z].astype(F32)

            @pl.when(z < nz - 1)
            def _():
                rdn_copy(z).wait_recv()
                acc[z] = acc[z] + rdn[z].astype(F32)

            moe_out[...] = acc[z].astype(BF16)

        def drain_moe():
            def sends(b, carry):
                @pl.when((b <= z) & (z < nz - 1))
                def _():
                    for d in range(nx):
                        for c in tok_up(b, d, lax.rem(x + nx - d, nx)):
                            c.wait_send()

                @pl.when((b >= z) & (z > 0))
                def _():
                    for d in range(nx):
                        for c in tok_dn(b, d, lax.rem(x + nx - d, nx)):
                            c.wait_send()

                @pl.when(b > z)
                def _():
                    rup_copy(b).wait_send()

                @pl.when(b < z)
                def _():
                    rdn_copy(b).wait_send()

                return carry

            lax.fori_loop(0, nz, sends, 0)
            for d in range(1, nx):
                res_copy(d).wait_send()
                for c in tok_x(d, x):
                    c.wait_send()

        start_first()
    else:
        start_first()
    for copy in meta_copies:
        copy.wait_recv()
    hot_step, hot_count = hot_steps()
    if dense:
        at_own, at_other, at_sum = (hot_count * n // 14 for n in (4, 6, 10))

        def early(s, carry):
            tok_step(s, carry)
            return hot_step(s, carry)

        lax.fori_loop(0, nz, early, 0)
        lax.fori_loop(nz, at_own, hot_step, 0)
        for copy in load_copies:
            copy.wait()
        acc[...] = apply(x)
        lax.fori_loop(max(nz, at_own), at_other, hot_step, 0)
        for d in range(1, nx):
            col = lax.rem(x + nx - d, nx)
            res[d - 1] = apply(col).astype(BF16)
            res_copy(d).start()
        lax.fori_loop(max(nz, at_other), at_sum, hot_step, 0)
        for d in range(1, nx):
            res_copy(d).wait_recv()
            acc[...] = acc[...] + xres[d - 1].astype(F32)

        def both(s, carry):
            hot_step(s, carry)
            return sum_step(s - at_sum, carry)

        lax.fori_loop(at_sum, hot_count, both, 0)
        finish_hot(range(1))
        lax.fori_loop(hot_count - at_sum, 2 * nz - 2, sum_step, 0)
        finish_hot(range(1, KINDS - 1))
        finish_sum()
        finish_hot(range(KINDS - 1, KINDS))
        drain_moe()
    else:
        lax.fori_loop(0, hot_count, hot_step, 0)
        finish_hot(range(KINDS))
    drain()


def shards(
    tokens,
    slot_choice,
    gate_fixed,
    expert_gate,
    expert_up,
    expert_down,
    next_weights,
    hot_expert,
    slot_take,
):
    sizes = tuple(lax.axis_size(a) for a in ("groups", "expert", "node", "inner"))
    ng, nz, nx, ni = sizes
    tok_rows, width = tokens.shape
    _, kinds, half, hidden = next_weights.shape
    assert kinds == KINDS and hot_expert.shape[0] == 2
    experts = nz * nx
    dense = experts * ni <= 2 * slot_choice.shape[1]
    part = half // (nx * ng)
    items = KINDS * (1 + ng)
    vmem, smem = (pl.BlockSpec(memory_space=s) for s in (pltpu.VMEM, pltpu.SMEM))
    dma = pltpu.SemaphoreType.DMA
    operands, specs = [next_weights, hot_expert, slot_take], [vmem, smem, smem]
    outs = [jax.ShapeDtypeStruct((1, KINDS, ni * half, hidden), BF16)]
    out_specs = [pl.BlockSpec(memory_space=pl.ANY)]
    dx, dg, di = max(nx - 1, 1), max(ng - 1, 1), max(ni - 1, 1)
    scratch = [
        pltpu.VMEM((8, 128), jnp.int32),
        pltpu.VMEM((dg, 8, 128), jnp.int32),
        pltpu.VMEM((di, 8, 128), jnp.int32),
        pltpu.VMEM((dx, KINDS, part, hidden), BF16),
        pltpu.VMEM((items, part, hidden), BF16),
        pltpu.VMEM((items, part, hidden), BF16),
        pltpu.VMEM((1 + ng, KINDS, nx, ng, part, hidden), BF16),
        pltpu.VMEM((KINDS, half, hidden), BF16),
        pltpu.VMEM((di, KINDS, half, hidden), BF16),
        dma((dg + di,)), dma((dg + di,)),
        dma((dx, KINDS)), dma((dx, KINDS)),
        dma((items,)), dma((items,)),
        dma((items,)), dma((items,)),
        dma((dx, items)), dma((dx, items)),
        dma((dg, items, nx)), dma((dg, items, nx)),
        dma((KINDS,)),
        dma((di, KINDS)), dma((di, KINDS)),
    ]
    if dense:
        owner = slot_choice // ni
        share = gate_fixed.astype(F32) * (1.0 / 65536.0)
        tall, wide = -(-experts // 8) * 8, -(-tok_rows // 128) * 128
        named = owner[None] == jnp.arange(tall, dtype=jnp.int32)[:, None, None]
        factors = jnp.sum(jnp.where(named, share[None], 0.0), axis=2)
        factors = jnp.pad(factors, ((0, 0), (0, wide - tok_rows)))
        operands += [tokens, factors, expert_gate, expert_up, expert_down]
        specs += [vmem] * 2 + [pl.BlockSpec(memory_space=pl.ANY)] * 3
        outs = [jax.ShapeDtypeStruct((tok_rows, width), BF16)] + outs
        out_specs = [vmem] + out_specs
        scratch += [
            pltpu.VMEM(expert_gate.shape, BF16),
            pltpu.VMEM(expert_up.shape, BF16),
            pltpu.VMEM(expert_down.shape, BF16),
            dma((3,)),
            pltpu.VMEM((nx, nz, tok_rows, width), BF16),
            pltpu.VMEM((nx, nz, tall, wide), F32),
            pltpu.VMEM((nz, tok_rows, width), F32),
            pltpu.VMEM((dx, nz, tok_rows, width), BF16),
            pltpu.VMEM((dx, nz, tok_rows, width), BF16),
            pltpu.VMEM((nz, tok_rows, width), BF16),
            pltpu.VMEM((nz, tok_rows, width), BF16),
            dma((nz, nx)), dma((nz, nx)), dma((nz, nx)), dma((nz, nx)), dma((dx,)), dma((dx,)),
            dma((nz, nx)), dma((nz, nx)), dma((nz, nx)), dma((nz, nx)), dma((dx,)), dma((dx,)),
            dma((dx,)), dma((dx,)),
            dma((nz,)), dma((nz,)), dma((nz,)), dma((nz,)),
        ]
    results = pl.pallas_call(
        functools.partial(kernel, sizes, dense),
        out_shape=outs,
        in_specs=specs,
        out_specs=out_specs,
        scratch_shapes=scratch,
        compiler_params=pltpu.CompilerParams(
            collective_id=0, has_side_effects=True, vmem_limit_bytes=56 * 2**20
        ),
    )(*operands)
    if dense:
        return tuple(results)
    moe_out = routed(tokens, slot_choice, gate_fixed, expert_gate, expert_up, expert_down)
    return moe_out, results[0]


def solution(mesh):
    tokens_spec = P(("groups", "expert", "node", "inner"), None)
    weights_spec = P(("expert", "node"), None, None)
    return jax.shard_map(
        shards,
        mesh=mesh,
        in_specs=(
            tokens_spec,
            tokens_spec,
            tokens_spec,
            weights_spec,
            weights_spec,
            weights_spec,
            P(("expert", "node"), None, "inner", None),
            P("groups"),
            P(("groups", "expert", "node", "inner")),
        ),
        out_specs=(tokens_spec, P(("groups", "expert", "node", "inner"), None, None, None)),
        check_vma=False,
    )
```

```python
import functools

import jax
import jax.numpy as jnp
from jax import lax
from jax.experimental import pallas as pl
from jax.experimental.pallas import tpu as pltpu
from jax.sharding import PartitionSpec as P

MESH = pl.DeviceIdType.MESH
BF16 = jnp.bfloat16
F32 = jnp.float32
KINDS = 3


def routed(tokens, slot_choice, gate_fixed, expert_gate, expert_up, expert_down):
    slot_count = lax.axis_size(("expert", "node", "inner"))
    tok_rows, model_width = tokens.shape
    pick_count = slot_choice.shape[1]
    capacity = max(2, 2 * tok_rows * pick_count // slot_count)
    flat_slot = slot_choice.reshape(-1)
    columns = jnp.arange(slot_count, dtype=jnp.int32)
    onehot = (flat_slot[:, None] == columns[None, :]).astype(jnp.int32)
    before = jnp.cumsum(onehot, axis=0) - onehot
    position = jnp.sum(before * onehot, axis=1)
    target = flat_slot * capacity + position
    source_rows = jnp.repeat(tokens, pick_count, axis=0)
    outgoing = jnp.zeros((slot_count * capacity, model_width), BF16).at[target].set(source_rows)
    outgoing = outgoing.reshape(slot_count, capacity, model_width)
    axes = ("expert", "node", "inner")
    block_rows = lax.all_to_all(outgoing, axes, split_axis=0, concat_axis=0, tiled=True)
    flat_rows = block_rows.reshape(-1, model_width)
    gate_value = jnp.dot(flat_rows, expert_gate[0], preferred_element_type=F32)
    up_value = jnp.dot(flat_rows, expert_up[0], preferred_element_type=F32)
    hidden = (jax.nn.silu(gate_value) * up_value).astype(BF16)
    result = jnp.dot(hidden, expert_down[0], preferred_element_type=F32).astype(BF16)
    returned = lax.all_to_all(
        result.reshape(block_rows.shape), axes, split_axis=0, concat_axis=0, tiled=True
    )
    back_rows = returned.reshape(slot_count * capacity, model_width)[target]
    factors = gate_fixed.reshape(-1).astype(F32) * (1.0 / 65536.0)
    weighted = back_rows.astype(F32) * factors[:, None]
    return jnp.sum(weighted.reshape(tok_rows, pick_count, model_width), axis=1).astype(BF16)


def pick(condition, yes, no):
    return lax.select_n(condition, no, yes)


def kernel(sizes, dense, *refs):
    ng, nz, nx, ni = sizes
    refs = list(refs)
    nw, hot, take = refs[:3]
    del refs[:3]
    if dense:
        tokens, factors, *w_in = refs[:5]
        del refs[:5]
        moe_out = refs.pop(0)
    out = refs.pop(0)
    (meta, meta_y, meta_i, xin, up, dn, full, own_out, peer_out) = refs[:9]
    del refs[:9]
    (m_send, m_recv, s1s, s1r, ups, upr, dns, dnr, xs, xr, ys, yr, os, ps, pr) = refs[:15]
    del refs[:15]

    g, z, x, i = (lax.axis_index(a) for a in ("groups", "expert", "node", "inner"))
    half = nw.shape[2]
    part = half // (nx * ng)
    experts = nz * nx
    unions = 1 + ng
    items = KINDS * unions
    above, below = lax.rem(z + 1, nz), lax.rem(z + nz - 1, nz)

    def rows(p, q):
        return pl.ds(pl.multiple_of((p * ng + q) * part, part), part)

    def remote(src, dst, send, recv, **where):
        return pltpu.make_async_remote_copy(
            src_ref=src, dst_ref=dst, send_sem=send, recv_sem=recv, device_id=where, device_id_type=MESH
        )

    barrier = pltpu.get_barrier_semaphore()

    def greet(**where):
        pl.semaphore_signal(barrier, inc=1, device_id=where, device_id_type=MESH)

    for d in range(1, nx):
        greet(node=lax.rem(x + d, nx))
    for d in range(1, ng):
        greet(groups=lax.rem(g + d, ng))
    for d in range(1, ni):
        greet(inner=lax.rem(i + d, ni))

    @pl.when(z > 0)
    def _():
        greet(expert=below)

    @pl.when(z < nz - 1)
    def _():
        greet(expert=above)

    ends = (z > 0).astype(jnp.int32) + (z < nz - 1).astype(jnp.int32)
    pl.semaphore_wait(barrier, nx - 1 + ng - 1 + ni - 1 + ends)

    last = experts - 1
    other = hot[0] + hot[1] - last
    last_place = pick(hot[0] == last, jnp.int32(0), jnp.int32(1))
    code = pick(take[0] == 2, jnp.int32(2), pick(take[0] == last_place, jnp.int32(0), jnp.int32(1)))
    line = lax.broadcasted_iota(jnp.int32, meta.shape, 0)
    meta[...] = jnp.where(line == 0, other, code)
    meta_copies = []
    for d in range(1, ng):
        n = len(meta_copies)
        meta_copies.append(
            remote(meta, meta_y.at[d - 1], m_send.at[n], m_recv.at[n], groups=lax.rem(g + d, ng))
        )
    for d in range(1, ni):
        n = len(meta_copies)
        meta_copies.append(
            remote(meta, meta_i.at[d - 1], m_send.at[n], m_recv.at[n], inner=lax.rem(i + d, ni))
        )
    for copy in meta_copies:
        copy.start()

    if dense:
        (w_gate, w_up, w_down, w_sem) = refs[:4]
        del refs[:4]
        load_copies = [
            pltpu.make_async_copy(src, dst, w_sem.at[n])
            for n, (src, dst) in enumerate(zip(w_in, (w_gate, w_up, w_down)))
        ]
        for copy in load_copies:
            copy.start()
        (tok, fac, acc, res, xres, rup, rdn) = refs[:7]
        (tus, tur, tds, tdr, txs, txr, fus, fur, fds, fdr, fxs, fxr, rxs, rxr, rus, rur, rds, rdr) = refs[7:]
        tok_rows = tokens.shape[0]

        def tok_up(b):
            return [
                remote(tok.at[x, b], tok.at[x, b], tus.at[b], tur.at[b], expert=above),
                remote(fac.at[x, b], fac.at[x, b], fus.at[b], fur.at[b], expert=above),
            ]

        def tok_dn(b):
            return [
                remote(tok.at[x, b], tok.at[x, b], tds.at[b], tdr.at[b], expert=below),
                remote(fac.at[x, b], fac.at[x, b], fds.at[b], fdr.at[b], expert=below),
            ]

        def tok_x(d, b, col):
            to = lax.rem(x + d, nx)
            return [
                remote(tok.at[col, b], tok.at[col, b], txs.at[d - 1, b], txr.at[d - 1, b], node=to),
                remote(fac.at[col, b], fac.at[col, b], fxs.at[d - 1, b], fxr.at[d - 1, b], node=to),
            ]

        tok[x, z] = tokens[...]
        fac[x, z] = factors[...]

        def tok_step(s, carry):
            bu, bd = z - s, z + s

            @pl.when(bu >= 0)
            def _():
                @pl.when(s > 0)
                def _():
                    for c in tok_up(bu):
                        c.wait_recv()

                @pl.when(z < nz - 1)
                def _():
                    for c in tok_up(bu):
                        c.start()

                for d in range(1, nx):
                    for c in tok_x(d, bu, x):
                        c.start()

            @pl.when(bd < nz)
            def _():
                @pl.when(s > 0)
                def _():
                    for c in tok_dn(bd):
                        c.wait_recv()

                @pl.when(z > 0)
                def _():
                    for c in tok_dn(bd):
                        c.start()

                @pl.when(s > 0)
                def _():
                    for d in range(1, nx):
                        for c in tok_x(d, bd, x):
                            c.start()

            return carry

    def first(d, k):
        to = lax.rem(x + d, nx)
        return remote(nw.at[0, k, rows(to, g)], xin.at[d - 1, k], s1s.at[d - 1, k], s1r.at[d - 1, k], node=to)

    def start_first():
        for k in range(KINDS):
            for d in range(1, nx):
                first(d, k).start()

    def up_copy(j):
        return remote(up.at[j], up.at[j], ups.at[j], upr.at[j], expert=above)

    def dn_copy(j):
        return remote(dn.at[j], dn.at[j], dns.at[j], dnr.at[j], expert=below)

    def x_copy(d, j, p):
        k, u = j // unions, j % unions
        spot = full.at[u, k, p, g]
        return remote(spot, spot, xs.at[d - 1, j], xr.at[d - 1, j], node=lax.rem(x + d, nx))

    def y_copy(d, j, p, q):
        k, u = j // unions, j % unions
        spot = full.at[u, k, p, q]
        return remote(spot, spot, ys.at[d - 1, j, p], yr.at[d - 1, j, p], groups=lax.rem(g + d, ng))

    def y_wanted(d, j):
        u = j % unions
        return (u == 0) | (u == 1 + lax.rem(g + d, ng))

    def y_start(j, p):
        for d in range(1, ng):
            @pl.when(y_wanted(d, j))
            def _():
                y_copy(d, j, p, g).start()

    def hot_steps():
        others = [other] + [jnp.max(meta_y[d - 1, 0:1, :]) for d in range(1, ng)]

        def owner(u):
            expert = jnp.int32(last)
            for d in range(ng):
                expert = pick(u == 1 + lax.rem(g + ng - d, ng), others[d], expert)
            return expert // nx, expert % nx

        def here(j):
            k, u = j // unions, j % unions
            oz, ox = owner(u)
            value = nw[0, k, rows(x, g), :]
            for d in range(1, nx):
                value = pick(ox == lax.rem(x + nx - d, nx), xin[d - 1, k], value)
            return oz, value

        def line_step(j, buffer, copy, first_one, last_one):
            @pl.when((j >= 0) & (j < items))
            def _():
                oz, value = here(j)

                @pl.when(first_one)
                def _():
                    buffer[j] = value

                @pl.when(jnp.logical_not(first_one))
                def _():
                    copy(j).wait_recv()
                    buffer[j] = pick(oz == z, value, buffer[j])

                @pl.when(jnp.logical_not(last_one))
                def _():
                    copy(j).start()

        lag = 2
        far, near = jnp.maximum(z, nz - 1 - z), jnp.minimum(z, nz - 1 - z)

        def step(s, carry):
            j1 = s - near

            @pl.when((j1 >= 0) & (j1 < items) & (j1 % unions == 0))
            def _():
                for d in range(1, nx):
                    first(d, j1 // unions).wait_recv()

            line_step(s - z, up, up_copy, z == 0, z == nz - 1)
            line_step(s - (nz - 1 - z), dn, dn_copy, z == nz - 1, z == 0)
            j = s - far

            @pl.when((j >= 0) & (j < items))
            def _():
                k, u = j // unions, j % unions
                oz, _ = owner(u)
                full[u, k, x, g] = pick(oz <= z, up[j], dn[j])
                for d in range(1, nx):
                    x_copy(d, j, x).start()
                y_start(j, x)

            j2 = j - lag

            @pl.when((j2 >= 0) & (j2 < items))
            def _():
                for d in range(1, nx):
                    p = lax.rem(x + nx - d, nx)
                    x_copy(d, j2, p).wait_recv()
                    y_start(j2, p)

            return carry

        return step, items + nz - 1 + lag

    def out_rows():
        return pl.ds(pl.multiple_of(i * half, half), half)

    def own_copy(k):
        return pltpu.make_async_copy(own_out.at[k], out.at[0, k, out_rows()], os.at[k])

    def peer_copy(d, k):
        to = lax.rem(i + d, ni)
        return remote(peer_out.at[d - 1, k], out.at[0, k, out_rows()], ps.at[d - 1, k], pr.at[d - 1, k], inner=to)

    def finish_hot(kinds):
        codes = [jnp.max(meta_i[d - 1, 1:2, :]) for d in range(1, ni)]
        for k in kinds:
            for d in range(1, ng):
                q = lax.rem(g + ng - d, ng)
                for p in range(nx):
                    y_copy(d, k * unions, p, q).wait_recv()
                    y_copy(d, k * unions + 1 + g, p, q).wait_recv()
            known = full[0, k].reshape(half, full.shape[-1])
            second = full[1 + g, k].reshape(half, full.shape[-1])

            def chosen(c):
                return pick(c == 2, jnp.zeros_like(known), pick(c == 0, known, second))

            for d in range(1, ni):
                peer_out[d - 1, k] = chosen(codes[ni - d - 1])
                peer_copy(d, k).start()
            own_out[k] = chosen(code)
            own_copy(k).start()

    def drain():
        for copy in meta_copies:
            copy.wait_send()
        for k in range(KINDS):
            for d in range(1, nx):
                first(d, k).wait_send()

        def sends(j, carry):
            @pl.when(z < nz - 1)
            def _():
                up_copy(j).wait_send()

            @pl.when(z > 0)
            def _():
                dn_copy(j).wait_send()

            for d in range(1, nx):
                x_copy(d, j, x).wait_send()
            for d in range(1, ng):
                @pl.when(y_wanted(d, j))
                def _():
                    for p in range(nx):
                        y_copy(d, j, p, g).wait_send()
            return carry

        lax.fori_loop(0, items, sends, 0)
        for k in range(KINDS):
            own_copy(k).wait()
            for d in range(1, ni):
                peer_copy(d, k).wait_send()
                peer_copy(d, k).wait_recv()

    if dense:
        def apply(col):
            count = nz * tok_rows
            block = tok[col].reshape(count, tok.shape[-1])
            gate_value = jnp.dot(block, w_gate[0], preferred_element_type=F32)
            up_value = jnp.dot(block, w_up[0], preferred_element_type=F32)
            hidden = gate_value / (1.0 + jnp.exp(-gate_value)) * up_value
            row = lax.broadcasted_iota(jnp.int32, (tok_rows, fac.shape[-1]), 0)
            column = lax.broadcasted_iota(jnp.int32, (tok_rows, fac.shape[-1]), 1)
            weights = []
            for b in range(nz):
                line_of = fac[col, b, pl.ds(z * nx + x, 1), :]
                weights.append(jnp.sum(jnp.where(row == column, line_of, 0.0), axis=1, keepdims=True))
            hidden = (hidden * jnp.concatenate(weights, axis=0)).astype(BF16)
            return jnp.dot(hidden, w_down[0], preferred_element_type=F32).reshape(nz, tok_rows, -1)

        def res_copy(d):
            return remote(res.at[d - 1], xres.at[d - 1], rxs.at[d - 1], rxr.at[d - 1], node=lax.rem(x + nx - d, nx))

        def rup_copy(b):
            return remote(rup.at[b], rup.at[b], rus.at[b], rur.at[b], expert=above)

        def rdn_copy(b):
            return remote(rdn.at[b], rdn.at[b], rds.at[b], rdr.at[b], expert=below)

        def sum_step(s, carry):
            iu, id_ = s - z, s - (nz - 1 - z)
            bu, bd = nz - 1 - iu, id_

            @pl.when((iu >= 0) & (bu > z))
            def _():
                @pl.when(z == 0)
                def _():
                    rup[bu] = acc[bu].astype(BF16)

                @pl.when(z > 0)
                def _():
                    rup_copy(bu).wait_recv()
                    rup[bu] = (acc[bu] + rup[bu].astype(F32)).astype(BF16)

                rup_copy(bu).start()

            @pl.when((id_ >= 0) & (bd < z))
            def _():
                @pl.when(z == nz - 1)
                def _():
                    rdn[bd] = acc[bd].astype(BF16)

                @pl.when(z < nz - 1)
                def _():
                    rdn_copy(bd).wait_recv()
                    rdn[bd] = (acc[bd] + rdn[bd].astype(F32)).astype(BF16)

                rdn_copy(bd).start()

            return carry

        def finish_sum():
            @pl.when(z > 0)
            def _():
                rup_copy(z).wait_recv()
                acc[z] = acc[z] + rup[z].astype(F32)

            @pl.when(z < nz - 1)
            def _():
                rdn_copy(z).wait_recv()
                acc[z] = acc[z] + rdn[z].astype(F32)

            moe_out[...] = acc[z].astype(BF16)

        def drain_moe():
            def sends(b, carry):
                @pl.when((b <= z) & (z < nz - 1))
                def _():
                    for c in tok_up(b):
                        c.wait_send()

                @pl.when((b >= z) & (z > 0))
                def _():
                    for c in tok_dn(b):
                        c.wait_send()

                for d in range(1, nx):
                    for c in tok_x(d, b, x):
                        c.wait_send()

                @pl.when(b > z)
                def _():
                    rup_copy(b).wait_send()

                @pl.when(b < z)
                def _():
                    rdn_copy(b).wait_send()

                return carry

            lax.fori_loop(0, nz, sends, 0)
            for d in range(1, nx):
                res_copy(d).wait_send()

        start_first()
    else:
        start_first()
    for copy in meta_copies:
        copy.wait_recv()
    hot_step, hot_count = hot_steps()
    if dense:
        at_own, at_other, at_sum = (hot_count * n // 14 for n in (4, 6, 10))

        def early(s, carry):
            tok_step(s, carry)
            return hot_step(s, carry)

        lax.fori_loop(0, nz, early, 0)
        lax.fori_loop(nz, at_own, hot_step, 0)
        for copy in load_copies:
            copy.wait()
        acc[...] = apply(x)
        lax.fori_loop(max(nz, at_own), at_other, hot_step, 0)
        for d in range(1, nx):
            col = lax.rem(x + nx - d, nx)
            for b in range(nz):
                for c in tok_x(d, b, col):
                    c.wait_recv()
            res[d - 1] = apply(col).astype(BF16)
            res_copy(d).start()
        lax.fori_loop(max(nz, at_other), at_sum, hot_step, 0)
        for d in range(1, nx):
            res_copy(d).wait_recv()
            acc[...] = acc[...] + xres[d - 1].astype(F32)

        def both(s, carry):
            hot_step(s, carry)
            return sum_step(s - at_sum, carry)

        lax.fori_loop(at_sum, hot_count, both, 0)
        lax.fori_loop(hot_count - at_sum, 2 * nz - 2, sum_step, 0)
        finish_hot(range(KINDS - 1))
        finish_sum()
        finish_hot(range(KINDS - 1, KINDS))
        drain_moe()
    else:
        lax.fori_loop(0, hot_count, hot_step, 0)
        finish_hot(range(KINDS))
    drain()


def shards(
    tokens,
    slot_choice,
    gate_fixed,
    expert_gate,
    expert_up,
    expert_down,
    next_weights,
    hot_expert,
    slot_take,
):
    sizes = tuple(lax.axis_size(a) for a in ("groups", "expert", "node", "inner"))
    ng, nz, nx, ni = sizes
    tok_rows, width = tokens.shape
    _, kinds, half, hidden = next_weights.shape
    assert kinds == KINDS and hot_expert.shape[0] == 2
    experts = nz * nx
    dense = experts * ni <= 2 * slot_choice.shape[1]
    part = half // (nx * ng)
    items = KINDS * (1 + ng)
    vmem, smem = (pl.BlockSpec(memory_space=s) for s in (pltpu.VMEM, pltpu.SMEM))
    dma = pltpu.SemaphoreType.DMA
    operands, specs = [next_weights, hot_expert, slot_take], [vmem, smem, smem]
    outs = [jax.ShapeDtypeStruct((1, KINDS, ni * half, hidden), BF16)]
    out_specs = [pl.BlockSpec(memory_space=pl.ANY)]
    dx, dg, di = max(nx - 1, 1), max(ng - 1, 1), max(ni - 1, 1)
    scratch = [
        pltpu.VMEM((8, 128), jnp.int32),
        pltpu.VMEM((dg, 8, 128), jnp.int32),
        pltpu.VMEM((di, 8, 128), jnp.int32),
        pltpu.VMEM((dx, KINDS, part, hidden), BF16),
        pltpu.VMEM((items, part, hidden), BF16),
        pltpu.VMEM((items, part, hidden), BF16),
        pltpu.VMEM((1 + ng, KINDS, nx, ng, part, hidden), BF16),
        pltpu.VMEM((KINDS, half, hidden), BF16),
        pltpu.VMEM((di, KINDS, half, hidden), BF16),
        dma((dg + di,)), dma((dg + di,)),
        dma((dx, KINDS)), dma((dx, KINDS)),
        dma((items,)), dma((items,)),
        dma((items,)), dma((items,)),
        dma((dx, items)), dma((dx, items)),
        dma((dg, items, nx)), dma((dg, items, nx)),
        dma((KINDS,)),
        dma((di, KINDS)), dma((di, KINDS)),
    ]
    if dense:
        owner = slot_choice // ni
        share = gate_fixed.astype(F32) * (1.0 / 65536.0)
        tall, wide = -(-experts // 8) * 8, -(-tok_rows // 128) * 128
        named = owner[None] == jnp.arange(tall, dtype=jnp.int32)[:, None, None]
        factors = jnp.sum(jnp.where(named, share[None], 0.0), axis=2)
        factors = jnp.pad(factors, ((0, 0), (0, wide - tok_rows)))
        operands += [tokens, factors, expert_gate, expert_up, expert_down]
        specs += [vmem] * 2 + [pl.BlockSpec(memory_space=pl.ANY)] * 3
        outs = [jax.ShapeDtypeStruct((tok_rows, width), BF16)] + outs
        out_specs = [vmem] + out_specs
        scratch += [
            pltpu.VMEM(expert_gate.shape, BF16),
            pltpu.VMEM(expert_up.shape, BF16),
            pltpu.VMEM(expert_down.shape, BF16),
            dma((3,)),
            pltpu.VMEM((nx, nz, tok_rows, width), BF16),
            pltpu.VMEM((nx, nz, tall, wide), F32),
            pltpu.VMEM((nz, tok_rows, width), F32),
            pltpu.VMEM((dx, nz, tok_rows, width), BF16),
            pltpu.VMEM((dx, nz, tok_rows, width), BF16),
            pltpu.VMEM((nz, tok_rows, width), BF16),
            pltpu.VMEM((nz, tok_rows, width), BF16),
            dma((nz,)), dma((nz,)), dma((nz,)), dma((nz,)), dma((dx, nz)), dma((dx, nz)),
            dma((nz,)), dma((nz,)), dma((nz,)), dma((nz,)), dma((dx, nz)), dma((dx, nz)),
            dma((dx,)), dma((dx,)),
            dma((nz,)), dma((nz,)), dma((nz,)), dma((nz,)),
        ]
    results = pl.pallas_call(
        functools.partial(kernel, sizes, dense),
        out_shape=outs,
        in_specs=specs,
        out_specs=out_specs,
        scratch_shapes=scratch,
        compiler_params=pltpu.CompilerParams(
            collective_id=0, has_side_effects=True, vmem_limit_bytes=56 * 2**20
        ),
    )(*operands)
    if dense:
        return tuple(results)
    moe_out = routed(tokens, slot_choice, gate_fixed, expert_gate, expert_up, expert_down)
    return moe_out, results[0]


def solution(mesh):
    tokens_spec = P(("groups", "expert", "node", "inner"), None)
    weights_spec = P(("expert", "node"), None, None)
    return jax.shard_map(
        shards,
        mesh=mesh,
        in_specs=(
            tokens_spec,
            tokens_spec,
            tokens_spec,
            weights_spec,
            weights_spec,
            weights_spec,
            P(("expert", "node"), None, "inner", None),
            P("groups"),
            P(("groups", "expert", "node", "inner")),
        ),
        out_specs=(tokens_spec, P(("groups", "expert", "node", "inner"), None, None, None)),
        check_vma=False,
    )
```
